512 devices in a mesh: pulse: 64 (over z, y), chan: 8 (over x, core).
Axes of the slice: x: 4, y: 8, z: 8, core: 2. Of those that a mesh axis runs over, the one named last changes fastest.
Arguments:
- echoes: bfloat16 [2, 8, 4096, 4096], P(None, 'chan', 'pulse'), may hold values from -6 to 6
- range_phase: float32 [512], replicated, may hold values from -3.140625 to 3.140625
- azimuth_rate: float32 [512], P('pulse'), may hold values from 1 to 4
- band_lo: int32 [64], P('pulse'), may hold values from 0 to 504, as said below
- band_hi: int32 [64], P('pulse'), may hold values from 8 to 512, as said below
- band_map: int32 [8], replicated, may hold values from 0 to 7, each once
- recon_filter: bfloat16 [8, 8, 2, 4096], replicated, may hold values from -1.5 to 1.5
Outputs:
- focused: float32 [2, 512, 32768], P(None, 'pulse', 'chan')
The draws below stay inside these ranges and needn't reach their ends.
Inputs may be any that keep to these rules, and one draw needn't show every extreme that they name: band_lo[b] lies in [b * 8 - 8, b * 8] and in the slab; the last block's band begins at the block; in some block strictly between the first and the last the band begins 8 bins before the block. band_hi[b] lies in [b * 8 + 8, b * 8 + 2 * 8] and in the slab; the first block's band ends at the block's end; in the same block as above the band ends 8 bins after it. `band_map`: a permutation.
All inputs are finite; a program needn't handle non-finite values.
Results may differ from the reference program's by a relative error of at most 0.0037.
Values may be sent and summed in bfloat16 or wider, within the bound.
No kernel may reach another device: no remote copies, remote signals or barrier semaphores. Data moves between devices by JAX's collectives and lax.ppermute only.
A program may use at most 128 MiB of HBM per device.

```python
import math
import jax
import jax.numpy as jnp
from jax import lax

NS = 4096
RB_DEV = 8
MIGRATION = 7
PULSES = 4096
NR = 512
CHANS = 8
SPECTRUM = 32768
N_PULSE = 64


def band_offsets(key):
    before = jax.random.randint(jax.random.fold_in(key, 11), (N_PULSE,), 0, RB_DEV + 1)
    after = jax.random.randint(jax.random.fold_in(key, 12), (N_PULSE,), 0, RB_DEV + 1)
    chosen = jax.random.randint(jax.random.fold_in(key, 13), (), 1, N_PULSE - 1)
    block_ids = jnp.arange(N_PULSE, dtype=jnp.int32)
    marked = block_ids == chosen
    before = jnp.where(marked, RB_DEV, before)
    after = jnp.where(marked, RB_DEV, after)
    before = jnp.where(block_ids == N_PULSE - 1, 0, before)
    after = jnp.where(block_ids == 0, 0, after)
    return (before.astype(jnp.int32), after.astype(jnp.int32))


def draw_band_lo(key, part):
    before, after = band_offsets(key)
    starts = jnp.arange(N_PULSE, dtype=jnp.int32) * RB_DEV
    return jnp.maximum(starts - before, 0).astype(jnp.int32)


def draw_band_hi(key, part):
    before, after = band_offsets(key)
    starts = jnp.arange(N_PULSE, dtype=jnp.int32) * RB_DEV
    return jnp.minimum(starts + RB_DEV + after, NR).astype(jnp.int32)


def steps_of(rng, dims, shards, low, top_value):
    gain = 1.0
    for axis_at, blocks in shards:
        steps = jax.random.uniform(jax.random.fold_in(jax.random.fold_in(rng, 6), axis_at), (blocks,), jnp.float32, low / len(shards), top_value / len(shards))
        gain = gain * jnp.repeat(jnp.exp(steps), dims[axis_at] // blocks).reshape((-1,) + (1,) * (len(dims) - 1 - axis_at))
    return gain


def gaussian(key, extent, scale, bound, pieces=(), held_as=jnp.bfloat16):
    values = scale * jax.random.normal(key, extent, jnp.float32)
    if pieces:
        values = values * steps_of(key, extent, pieces, -0.22, 0.18)
    return jnp.clip(values, -bound, bound).astype(held_as)


def setup_inputs(seed: int = 0) -> dict:
    splits = jax.random.split(jax.random.key(seed), 8)
    return {
        "echoes": gaussian(splits[0], (2, CHANS, PULSES, NS), 1.0, 6.0, ((1, 8), (2, 64))),
        "range_phase": jnp.clip(jax.random.uniform(splits[1], (NR,), jnp.float32, -3.140625, 3.140625), -3.140625, 3.140625),
        "azimuth_rate": jnp.clip(jnp.exp(math.log(4.0) - 1.3862944 * jax.random.uniform(splits[2], (NR,), jnp.float32) ** steps_of(splits[2], (NR,), ((0, 64),), -0.2, 0.2)), 1.0, 4.0),
        "band_lo": draw_band_lo(jax.random.fold_in(splits[7], 71), 0),
        "band_hi": draw_band_hi(jax.random.fold_in(splits[7], 71), 0),
        "band_map": jax.random.permutation(splits[5], CHANS).astype(jnp.int32),
        "recon_filter": gaussian(splits[6], (CHANS, CHANS, 2, PULSES), (2 * CHANS) ** -0.5, 1.5),
    }


curvature = 300.0
highest = lax.Precision.HIGHEST

def angle_table(rows, cols, length):
    index_prod = lax.broadcasted_iota(jnp.int32, (rows, cols), 0) * lax.broadcasted_iota(jnp.int32, (rows, cols), 1)
    return (index_prod % length).astype(jnp.float32) * (2.0 * math.pi / length)

def rotate(real_x, imag_x, cos_part, sin_part):
    return (real_x * cos_part - imag_x * sin_part, imag_x * cos_part + real_x * sin_part)

def hat_weights(doppler, range_bins, total_bins):
    spread = 2.0 * jnp.square(2.0 * doppler)[None, :] * (0.5 + 0.5 * range_bins[:, None] / total_bins) - 1.0
    centre = (RB_DEV + lax.iota(jnp.float32, RB_DEV))[:, None] + MIGRATION * spread
    source_bins = lax.iota(jnp.float32, 3 * RB_DEV)
    return jnp.maximum(0.0, 1.0 - jnp.abs(source_bins[:, None, None] - centre[None]))

def reference(echoes, range_phase, azimuth_rate, band_lo, band_hi, band_map, recon_filter):
    cos_table = jnp.cos(angle_table(NS, NR, NS)).astype(jnp.bfloat16)
    sin_table = jnp.sin(angle_table(NS, NR, NS)).astype(jnp.bfloat16)
    norm_scale = 1.0 / math.sqrt(NS)
    ref_cos = jnp.cos(range_phase)
    ref_sin = jnp.sin(range_phase)

    def compress(channel):
        echo_re = lax.dynamic_index_in_dim(echoes[0], channel, 0, keepdims=False)
        echo_im = lax.dynamic_index_in_dim(echoes[1], channel, 0, keepdims=False)
        comp_re = (jnp.dot(echo_re, cos_table, preferred_element_type=jnp.float32) + jnp.dot(echo_im, sin_table, preferred_element_type=jnp.float32)) * norm_scale
        comp_im = (jnp.dot(echo_im, cos_table, preferred_element_type=jnp.float32) - jnp.dot(echo_re, sin_table, preferred_element_type=jnp.float32)) * norm_scale
        return jnp.stack(rotate(comp_re, comp_im, ref_cos, ref_sin))
    compressed = lax.map(compress, jnp.arange(CHANS, dtype=jnp.int32))
    padded = jnp.pad(compressed, ((0, 0), (0, 0), (0, 0), (RB_DEV, RB_DEV)))
    filters = recon_filter.astype(jnp.float32)

    def focus(block):
        window = lax.dynamic_slice_in_dim(padded, (block * RB_DEV).astype(jnp.int32), 3 * RB_DEV, 3)
        slab_bins = block * RB_DEV - RB_DEV + lax.iota(jnp.int32, 3 * RB_DEV)
        inside = ((slab_bins >= band_lo[block]) & (slab_bins < band_hi[block])).astype(jnp.float32)
        window = window * inside
        series = lax.complex(window[:, 0], window[:, 1])
        spectra = jnp.fft.fft(series, axis=1) / math.sqrt(PULSES)
        spec_re = jnp.real(spectra).transpose(0, 2, 1)
        spec_im = jnp.imag(spectra).transpose(0, 2, 1)
        spec_re = lax.optimization_barrier(spec_re.astype(jnp.bfloat16)).astype(jnp.float32)
        spec_im = lax.optimization_barrier(spec_im.astype(jnp.bfloat16)).astype(jnp.float32)
        rates = lax.dynamic_slice_in_dim(azimuth_rate, (block * RB_DEV).astype(jnp.int32), RB_DEV)
        range_bins = (block * RB_DEV + lax.iota(jnp.int32, RB_DEV)).astype(jnp.float32)
        doppler_bins = lax.iota(jnp.int32, PULSES)
        bands = []
        for source in range(CHANS):
            doppler = (band_map[source] * PULSES + doppler_bins).astype(jnp.float32) / SPECTRUM - 0.5
            filt_re = filters[source, :, 0]
            filt_im = filters[source, :, 1]
            merged_re = jnp.einsum('cj,cwj->wj', filt_re, spec_re, precision=highest) - jnp.einsum('cj,cwj->wj', filt_im, spec_im, precision=highest)
            merged_im = jnp.einsum('cj,cwj->wj', filt_re, spec_im, precision=highest) + jnp.einsum('cj,cwj->wj', filt_im, spec_re, precision=highest)
            weights = hat_weights(doppler, range_bins, NR)
            moved_re = jnp.einsum('wj,wqj->qj', merged_re, weights, precision=highest)
            moved_im = jnp.einsum('wj,wqj->qj', merged_im, weights, precision=highest)
            phase_angle = -curvature * jnp.square(doppler)[None, :] / rates[:, None]
            band_re, band_im = rotate(moved_re, moved_im, jnp.cos(phase_angle), jnp.sin(phase_angle))
            bands.append(jnp.stack([band_re, band_im]))
        stacked = jnp.stack(bands)
        one_hot = (band_map[:, None] == lax.iota(jnp.int32, CHANS)[None, :]).astype(jnp.float32)
        placed = jnp.einsum('kl,kprj->lprj', one_hot, stacked, precision=highest)
        full = placed.transpose(1, 2, 0, 3).reshape(2, RB_DEV, SPECTRUM)
        image = jnp.fft.ifft(lax.complex(full[0], full[1]), axis=1) * math.sqrt(SPECTRUM)
        image_re = jnp.real(image).reshape(RB_DEV, PULSES, CHANS).transpose(0, 2, 1).reshape(RB_DEV, SPECTRUM)
        image_im = jnp.imag(image).reshape(RB_DEV, PULSES, CHANS).transpose(0, 2, 1).reshape(RB_DEV, SPECTRUM)
        return jnp.stack([image_re, image_im])
    focused_blocks = lax.map(focus, jnp.arange(N_PULSE, dtype=jnp.int32))
    return focused_blocks.transpose(1, 0, 2, 3).reshape(2, NR, SPECTRUM)
```

```python
import math

import jax
import jax.numpy as jnp
import numpy as np
from jax import lax
from jax.experimental import pallas as pl
from jax.experimental.pallas import tpu as pltpu
from jax.sharding import PartitionSpec as P

NS = 4096
RB_DEV = 8
MIGRATION = 7
PULSES = 4096
NR = 512
CHANS = 8
SPECTRUM = 32768
N_PULSE = 64

RADIX = 4
FOLD = NS // RADIX
LANES = 128
ROWS = PULSES // LANES
OWN = ROWS // CHANS
PULSES_DEV = PULSES // N_PULSE
curvature = 300.0

f32 = jnp.float32
bf16 = jnp.bfloat16


def split_np(values):
    high = np.asarray(values, np.float32).astype(bf16)
    low = (values - high.astype(np.float64)).astype(np.float32).astype(bf16)
    return high, low


def range_tables():
    tables = []
    sample = np.arange(FOLD)
    for rho in range(RADIX):
        bins = np.array([8 * block + 4 * h + rho for h in range(2) for block in range(N_PULSE)])
        angle = (bins[:, None] * sample[None, :]) % NS * (2.0 * math.pi / NS)
        tables.append(np.concatenate([np.cos(angle), np.sin(angle)], axis=0))
    return np.stack(tables).astype(np.float32).astype(bf16)


def row_tables():
    digit = np.arange(ROWS)
    angle = (digit[:, None] * digit[None, :]) % ROWS * (2.0 * math.pi / ROWS)
    eye = np.eye(RB_DEV)
    cos_hi, cos_lo = split_np(np.kron(np.cos(angle), eye))
    sin_hi, sin_lo = split_np(np.kron(np.sin(angle), eye))
    return np.concatenate([cos_hi, sin_hi, cos_lo, sin_lo], axis=0)


def lane_tables():
    digit = np.arange(LANES)
    angle = (digit[:, None] * digit[None, :]) % LANES * (2.0 * math.pi / LANES)
    cos_m, sin_m = np.cos(angle), np.sin(angle)
    high, low = split_np(np.block([[cos_m, -sin_m], [sin_m, cos_m]]))
    return np.concatenate([high, low], axis=1)


def twiddle_tables():
    angle = np.arange(ROWS)[:, None] * np.arange(LANES)[None, :] * (2.0 * math.pi / PULSES)
    angle = np.repeat(angle, RB_DEV, axis=0)
    return np.concatenate([np.cos(angle), np.sin(angle)], axis=1).astype(np.float32)


def dot(left, right):
    return jnp.dot(left, right, preferred_element_type=f32)


def split(values):
    high = values.astype(bf16)
    return high, (values - high.astype(f32)).astype(bf16)


def lane_index(shape):
    return lax.broadcasted_iota(jnp.int32, shape, 1)


def compress_kernel(echo_ref, table_ref, out_ref, folded, bins):
    rho = pl.program_id(0)

    def quarters(part):
        return [
            echo_ref[part, 0, :, a * FOLD : (a + 1) * FOLD].astype(f32) for a in range(RADIX)
        ]

    def put(part, values):
        high, low = split(values)
        folded[part * 64 : part * 64 + 64, :] = high
        folded[128 + part * 64 : 128 + part * 64 + 64, :] = low

    for residue in range(RADIX):

        @pl.when(rho == residue)
        def _():
            re0, re1, re2, re3 = quarters(0)
            im0, im1, im2, im3 = quarters(1)
            if residue == 0:
                put(0, (re0 + re2) + (re1 + re3))
                put(1, (im0 + im2) + (im1 + im3))
            elif residue == 1:
                put(0, (re0 - re2) + (im1 - im3))
                put(1, (im0 - im2) - (re1 - re3))
            elif residue == 2:
                put(0, (re0 + re2) - (re1 + re3))
                put(1, (im0 + im2) - (im1 + im3))
            else:
                put(0, (re0 - re2) - (im1 - im3))
                put(1, (im0 - im2) + (re1 - re3))
            sums = lax.dot_general(
                table_ref[0], folded[...], (((1,), (1,)), ((), ())), preferred_element_type=f32
            )
            sums = sums[:, :LANES] + sums[:, LANES:]
            cos_sum, sin_sum = sums[:128], sums[128:]
            sign = jnp.where(lane_index((128, LANES)) < 64, 1.0, -1.0)
            comp = cos_sum + sign * pltpu.roll(sin_sum, 64, 1)
            for h in range(2):
                bins[pl.ds(4 * h + residue, N_PULSE, stride=RB_DEV), :] = comp[
                    h * N_PULSE : (h + 1) * N_PULSE
                ]

    @pl.when(rho == RADIX - 1)
    def _():
        own = bins[...].astype(bf16).reshape(N_PULSE, RB_DEV, LANES)
        edge = jnp.zeros((1, RB_DEV, LANES), bf16)
        out_ref[0:1, :, 0:LANES] = edge
        out_ref[1:N_PULSE, :, 0:LANES] = own[: N_PULSE - 1]
        out_ref[:, :, LANES : 2 * LANES] = own
        out_ref[0 : N_PULSE - 1, :, 2 * LANES :] = own[1:]
        out_ref[N_PULSE - 1 :, :, 2 * LANES :] = edge


def compress(echoes, tables):
    return pl.pallas_call(
        compress_kernel,
        grid=(RADIX,),
        in_specs=[
            pl.BlockSpec((2, 1, PULSES_DEV, NS), lambda rho: (0, 0, 0, 0)),
            pl.BlockSpec((1, 256, FOLD), lambda rho: (rho, 0, 0)),
        ],
        out_specs=pl.BlockSpec((N_PULSE, RB_DEV, 3 * LANES), lambda rho: (0, 0, 0)),
        out_shape=jax.ShapeDtypeStruct((N_PULSE, RB_DEV, 3 * LANES), bf16),
        scratch_shapes=[pltpu.VMEM((256, FOLD), bf16), pltpu.VMEM((NR, LANES), f32)],
        compiler_params=pltpu.CompilerParams(vmem_limit_bytes=32 << 20),
        cost_estimate=pl.CostEstimate(
            flops=2 * RADIX * 256 * 256 * FOLD, bytes_accessed=4 << 20, transcendentals=0
        ),
        name="compress",
    )(echoes, tables)


def spectra_kernel(turned_ref, rows_ref, lanes_ref, twiddle_ref, gain_ref, out_ref):
    low_half = lane_index((256, LANES)) < 64
    tw_cos, tw_sin = twiddle_ref[:, :LANES], twiddle_ref[:, LANES:]
    table_hi, table_lo = lanes_ref[:, :256], lanes_ref[:, 256:]
    for group in range(3):
        taken = turned_ref[:, :, group * LANES : (group + 1) * LANES].astype(f32)
        pairs = taken.reshape(ROWS, 2, RB_DEV, LANES)
        even = pairs[:, 0].reshape(256, LANES)
        odd = pairs[:, 1].reshape(256, LANES)
        real_x = jnp.where(low_half, even, pltpu.roll(odd, 64, 1))
        imag_x = jnp.where(low_half, pltpu.roll(even, 64, 1), odd)
        samples = jnp.concatenate([real_x, imag_x], axis=1).astype(bf16)
        turned = dot(rows_ref[...], samples)
        cos_sum = turned[0:256] + turned[512:768]
        sin_sum = turned[256:512] + turned[768:1024]
        real_y = cos_sum[:, :LANES] + sin_sum[:, LANES:]
        imag_y = cos_sum[:, LANES:] - sin_sum[:, :LANES]
        real_z = real_y * tw_cos + imag_y * tw_sin
        imag_z = imag_y * tw_cos - real_y * tw_sin
        gain_re = gain_ref[0, group][None]
        gain_im = gain_ref[1, group][None]
        real_z = real_z.reshape(ROWS, RB_DEV, LANES)
        imag_z = imag_z.reshape(ROWS, RB_DEV, LANES)
        real_w = (real_z * gain_re - imag_z * gain_im).reshape(256, LANES)
        imag_w = (imag_z * gain_re + real_z * gain_im).reshape(256, LANES)
        high, low = split(jnp.concatenate([real_w, imag_w], axis=1))
        result = dot(high, table_hi) + (dot(low, table_hi) + dot(high, table_lo))
        out_ref[:, group * 32 : (group + 1) * 32, :] = result.astype(bf16).reshape(
            CHANS, 32, 256
        )


def spectra(turned, rows_table, lanes_table, twiddle, gain):
    return pl.pallas_call(
        spectra_kernel,
        out_shape=jax.ShapeDtypeStruct((CHANS, 96, 256), bf16),
        compiler_params=pltpu.CompilerParams(vmem_limit_bytes=32 << 20),
        cost_estimate=pl.CostEstimate(
            flops=6 * 256 * 256 * 1792, bytes_accessed=2 << 20, transcendentals=0
        ),
        name="spectra",
    )(turned, rows_table, lanes_table, twiddle, gain)


def prepare_kernel(
    scalars, rate_ref, filter_ref, filt_ref, cos_ref, sin_ref, base_ref, lanes_ref, twiddle_ref
):
    chan = scalars[CHANS]
    block = scalars[CHANS + 1]
    shape = (OWN * RB_DEV, LANES)
    row = lax.broadcasted_iota(jnp.int32, shape, 0)
    lane = lax.broadcasted_iota(jnp.int32, shape, 1)
    doppler_bin = 32 * lane + OWN * chan + lax.shift_right_logical(row, 3)
    q = jnp.bitwise_and(row, 7)
    bins = (block * RB_DEV + q).astype(f32)
    slope = 0.5 + 0.5 * bins / NR
    place = (RB_DEV + q).astype(f32)
    rates = jnp.concatenate([rate_ref[...]] * OWN, axis=0)
    for k in range(CHANS):
        doppler = (scalars[k] * PULSES + doppler_bin).astype(f32) / SPECTRUM - 0.5
        spread = 2.0 * jnp.square(2.0 * doppler) * slope - 1.0
        base_ref[k] = place - (place + MIGRATION * spread)
        phase = -curvature * jnp.square(doppler) / rates
        cos_ref[k] = jnp.cos(phase)
        sin_ref[k] = jnp.sin(phase)
    pick_x = lax.broadcasted_iota(jnp.int32, (1024, LANES), 0)
    pick_y = lax.broadcasted_iota(jnp.int32, (1024, LANES), 1)
    wanted = 32 * jnp.bitwise_and(pick_y, 31) + OWN * chan + lax.shift_right_logical(pick_y, 5)
    pick = jnp.where(pick_x == wanted, 1.0, 0.0).astype(bf16)
    quarter = lax.shift_right_logical(lane_index((128, LANES)), 5)
    picked = [dot(filter_ref[:, 1024 * t : 1024 * (t + 1)], pick) for t in range(4)]
    for digit in range(OWN):
        total = jnp.zeros((128, LANES), f32)
        for t in range(4):
            moved = picked[t]
            if t != digit:
                moved = pltpu.roll(moved, (32 * (t - digit)) % LANES, 1)
            total = jnp.where(quarter == t, moved, total)
        filt_ref[digit] = total
    square = (LANES, LANES)
    j_hi = lax.broadcasted_iota(jnp.int32, square, 0)
    m_lo = lax.broadcasted_iota(jnp.int32, square, 1)
    turns = jnp.bitwise_and(8 * j_hi * m_lo + j_hi * chan, 1023)
    angle = turns.astype(f32) * (2.0 * math.pi / 1024)
    cos_hi, cos_lo = split(jnp.cos(angle))
    sin_hi, sin_lo = split(jnp.sin(angle))
    for at, (cos_m, sin_m) in enumerate(((cos_hi, sin_hi), (cos_lo, sin_lo))):
        left, mid, right = 256 * at, 256 * at + LANES, 256 * at + 256
        lanes_ref[:LANES, left:mid] = cos_m
        lanes_ref[:LANES, mid:right] = sin_m
        lanes_ref[LANES:, left:mid] = -sin_m
        lanes_ref[LANES:, mid:right] = cos_m
    small = (ROWS, LANES)
    j_lo = lax.broadcasted_iota(jnp.int32, small, 0)
    m_low = lax.broadcasted_iota(jnp.int32, small, 1)
    angle = (j_lo * (8 * m_low + chan)).astype(f32) * (2.0 * math.pi / SPECTRUM)
    scale = 1.0 / math.sqrt(SPECTRUM)
    for at, values in enumerate((jnp.cos(angle) * scale, jnp.sin(angle) * scale)):
        full = jnp.broadcast_to(values[:, None, :], (ROWS, RB_DEV, LANES)).reshape(256, LANES)
        twiddle_ref[:, at * LANES : (at + 1) * LANES] = full


def prepare(scalars, rates, filters):
    vmem = pl.BlockSpec(memory_space=pltpu.VMEM)
    return pl.pallas_call(
        prepare_kernel,
        in_specs=[pl.BlockSpec(memory_space=pltpu.SMEM), vmem, vmem],
        out_shape=(
            jax.ShapeDtypeStruct((OWN, 128, LANES), f32),
            jax.ShapeDtypeStruct((CHANS, OWN * RB_DEV, LANES), f32),
            jax.ShapeDtypeStruct((CHANS, OWN * RB_DEV, LANES), f32),
            jax.ShapeDtypeStruct((CHANS, OWN * RB_DEV, LANES), f32),
            jax.ShapeDtypeStruct((256, 512), bf16),
            jax.ShapeDtypeStruct((256, 256), f32),
        ),
        compiler_params=pltpu.CompilerParams(vmem_limit_bytes=32 << 20),
        cost_estimate=pl.CostEstimate(
            flops=1 << 29, bytes_accessed=2 << 20, transcendentals=1 << 18
        ),
        name="prepare",
    )(scalars, rates, filters)


def fft8(values):
    def add(u, v):
        return (u[0] + v[0], u[1] + v[1])

    def sub(u, v):
        return (u[0] - v[0], u[1] - v[1])

    def times_i(u):
        return (-u[1], u[0])

    half = math.sqrt(0.5)

    def fft4(v0, v1, v2, v3):
        e0, e1 = add(v0, v2), sub(v0, v2)
        o0, o1 = add(v1, v3), times_i(sub(v1, v3))
        return [add(e0, o0), add(e1, o1), sub(e0, o0), sub(e1, o1)]

    even = fft4(values[0], values[2], values[4], values[6])
    odd = fft4(values[1], values[3], values[5], values[7])
    odd[1] = ((odd[1][0] - odd[1][1]) * half, (odd[1][0] + odd[1][1]) * half)
    odd[2] = times_i(odd[2])
    odd[3] = ((-odd[3][0] - odd[3][1]) * half, (odd[3][0] - odd[3][1]) * half)
    return [add(e, o) for e, o in zip(even, odd)] + [sub(e, o) for e, o in zip(even, odd)]


def merge_kernel(
    scalars, gathered_ref, filt_ref, cos_ref, sin_ref, base_ref, out_ref, wide, merged, bands
):
    wide[...] = gathered_ref[...].astype(f32)

    def one_band(k, carry):
        band = scalars[k]
        for digit in range(OWN):
            rows = slice(digit * RB_DEV, (digit + 1) * RB_DEV)
            filters = filt_ref[digit, pl.ds(pl.multiple_of(k * 16, 16), 16), :]
            sums_re = [None] * 3
            sums_im = [None] * 3
            for c in range(CHANS):
                f_re = jnp.broadcast_to(filters[2 * c : 2 * c + 1], (RB_DEV, LANES))
                f_im = jnp.broadcast_to(filters[2 * c + 1 : 2 * c + 2], (RB_DEV, LANES))
                for group in range(3):
                    at = group * 32 + digit * RB_DEV
                    s_re = wide[c, at : at + RB_DEV, :LANES]
                    s_im = wide[c, at : at + RB_DEV, LANES:]
                    part_re = f_re * s_re - f_im * s_im
                    part_im = f_re * s_im + f_im * s_re
                    sums_re[group] = part_re if c == 0 else sums_re[group] + part_re
                    sums_im[group] = part_im if c == 0 else sums_im[group] + part_im
            for group in range(3):
                span = slice(group * RB_DEV, (group + 1) * RB_DEV)
                merged[digit, 0, span, :] = sums_re[group]
                merged[digit, 1, span, :] = sums_im[group]
            base = base_ref[k, rows, :]
            moved_re = None
            for step in range(-MIGRATION, MIGRATION + 1):
                weight = jnp.maximum(0.0, 1.0 - jnp.abs(base + float(step)))
                first = RB_DEV + step
                part_re = weight * merged[digit, 0, first : first + RB_DEV, :]
                part_im = weight * merged[digit, 1, first : first + RB_DEV, :]
                moved_re = part_re if moved_re is None else moved_re + part_re
                moved_im = part_im if step == -MIGRATION else moved_im + part_im
            cos_p = cos_ref[k, rows, :]
            sin_p = sin_ref[k, rows, :]
            bands[band, 0, rows, :] = moved_re * cos_p - moved_im * sin_p
            bands[band, 1, rows, :] = moved_im * cos_p + moved_re * sin_p
        return carry

    lax.fori_loop(0, CHANS, one_band, 0)
    for half in range(OWN * RB_DEV // 16):
        rows = slice(half * 16, half * 16 + 16)
        results = fft8([(bands[k, 0, rows, :], bands[k, 1, rows, :]) for k in range(CHANS)])
        for a in range(CHANS):
            out_ref[a, rows, :LANES] = results[a][0].astype(bf16)
            out_ref[a, rows, LANES:] = results[a][1].astype(bf16)


def merge(scalars, gathered, filt, cos_p, sin_p, base):
    vmem = pl.BlockSpec(memory_space=pltpu.VMEM)
    return pl.pallas_call(
        merge_kernel,
        in_specs=[pl.BlockSpec(memory_space=pltpu.SMEM)] + [vmem] * 5,
        out_shape=jax.ShapeDtypeStruct((CHANS, OWN * RB_DEV, 256), bf16),
        scratch_shapes=[
            pltpu.VMEM((CHANS, 96, 256), f32),
            pltpu.VMEM((OWN, 2, 3 * RB_DEV, LANES), f32),
            pltpu.VMEM((CHANS, 2, OWN * RB_DEV, LANES), f32),
        ],
        compiler_params=pltpu.CompilerParams(vmem_limit_bytes=32 << 20),
        cost_estimate=pl.CostEstimate(flops=1 << 24, bytes_accessed=2 << 20, transcendentals=0),
        name="merge",
    )(scalars, gathered, filt, cos_p, sin_p, base)


def image_kernel(combined_ref, rows_ref, lanes_ref, twiddle_ref, out_ref):
    combined = combined_ref[...].reshape(256, 256)
    turned = dot(combined, lanes_ref[...])
    turned = turned[:, :256] + turned[:, 256:]
    real_y, imag_y = turned[:, :LANES], turned[:, LANES:]
    tw_cos, tw_sin = twiddle_ref[:, :LANES], twiddle_ref[:, LANES:]
    real_z = real_y * tw_cos - imag_y * tw_sin
    imag_z = imag_y * tw_cos + real_y * tw_sin
    high, low = split(jnp.concatenate([real_z, imag_z], axis=1))
    wide = dot(rows_ref[...], high)
    rest = dot(rows_ref[0:512], low)
    cos_sum = wide[0:256] + (wide[512:768] + rest[0:256])
    sin_sum = wide[256:512] + (wide[768:1024] + rest[256:512])
    real_x = cos_sum[:, :LANES] - sin_sum[:, LANES:]
    imag_x = cos_sum[:, LANES:] + sin_sum[:, :LANES]
    for m_hi in range(ROWS):
        rows = slice(m_hi * RB_DEV, (m_hi + 1) * RB_DEV)
        cols = slice(m_hi * LANES, (m_hi + 1) * LANES)
        out_ref[0, :, cols] = real_x[rows]
        out_ref[1, :, cols] = imag_x[rows]


def image(combined, rows_table, lanes_table, twiddle):
    return pl.pallas_call(
        image_kernel,
        out_shape=jax.ShapeDtypeStruct((2, RB_DEV, PULSES), f32),
        compiler_params=pltpu.CompilerParams(vmem_limit_bytes=32 << 20),
        cost_estimate=pl.CostEstimate(
            flops=2 * 256 * 256 * 2048, bytes_accessed=2 << 20, transcendentals=0
        ),
        name="image",
    )(combined, rows_table, lanes_table, twiddle)


def window_gain(range_phase, band_lo, band_hi, block_index):
    slab_bins = block_index * RB_DEV - RB_DEV + lax.iota(jnp.int32, 3 * RB_DEV)
    inside = (slab_bins >= band_lo[0]) & (slab_bins < band_hi[0])
    scale = jnp.where(inside, 1.0 / math.sqrt(NS * PULSES), 0.0)
    phase = lax.dynamic_slice(
        jnp.pad(range_phase, (RB_DEV, RB_DEV)), (block_index * RB_DEV,), (3 * RB_DEV,)
    )
    gain = jnp.stack([scale * jnp.cos(phase), scale * jnp.sin(phase)])
    return jnp.broadcast_to(gain.reshape(2, 3, RB_DEV, 1), (2, 3, RB_DEV, LANES))


def per_device(echoes, range_phase, azimuth_rate, band_lo, band_hi, band_map, recon_filter):
    block_index = lax.axis_index("pulse").astype(jnp.int32)
    own_index = lax.axis_index("chan").astype(jnp.int32)
    scalars = jnp.concatenate([band_map, jnp.stack([own_index, block_index])])
    rows_table = jnp.asarray(row_tables())
    windows = compress(echoes, jnp.asarray(range_tables()))
    turned = lax.all_to_all(windows, "pulse", split_axis=0, concat_axis=0, tiled=True)
    gain = window_gain(range_phase, band_lo, band_hi, block_index)
    rates = jnp.broadcast_to(azimuth_rate[:, None], (RB_DEV, LANES))
    filt, cos_p, sin_p, base, last_lanes, last_twiddle = prepare(
        scalars, rates, recon_filter.reshape(2 * CHANS * CHANS, PULSES)
    )
    doppler = spectra(
        turned, rows_table, jnp.asarray(lane_tables()), jnp.asarray(twiddle_tables()), gain
    )
    gathered = lax.all_to_all(doppler, "chan", split_axis=0, concat_axis=0, tiled=True)
    summed = merge(scalars, gathered, filt, cos_p, sin_p, base)
    combined = lax.all_to_all(summed, "chan", split_axis=0, concat_axis=0, tiled=True)
    return image(combined, rows_table, last_lanes, last_twiddle)


def solution(mesh):
    in_specs = (P(None, "chan", "pulse", None), P(), P("pulse"), P("pulse"), P("pulse"), P(), P())
    out_specs = P(None, "pulse", "chan")
    return jax.shard_map(
        per_device, mesh=mesh, in_specs=in_specs, out_specs=out_specs, check_vma=False
    )
```

```python
import math

import jax
import jax.numpy as jnp
import numpy as np
from jax import lax
from jax.experimental import pallas as pl
from jax.experimental.pallas import tpu as pltpu
from jax.sharding import PartitionSpec as P

NS = 4096
RB_DEV = 8
MIGRATION = 7
PULSES = 4096
NR = 512
CHANS = 8
SPECTRUM = 32768
N_PULSE = 64

RADIX = 4
FOLD = NS // RADIX
LANES = 128
ROWS = PULSES // LANES
OWN = ROWS // CHANS
PULSES_DEV = PULSES // N_PULSE
curvature = 300.0

f32 = jnp.float32
bf16 = jnp.bfloat16


def split_np(values):
    high = np.asarray(values, np.float32).astype(bf16)
    low = (values - high.astype(np.float64)).astype(np.float32).astype(bf16)
    return high, low


def range_tables():
    tables = []
    sample = np.arange(FOLD)
    for rho in range(RADIX):
        bins = np.array([8 * block + 4 * h + rho for h in range(2) for block in range(N_PULSE)])
        angle = (bins[:, None] * sample[None, :]) % NS * (2.0 * math.pi / NS)
        tables.append(np.concatenate([np.cos(angle), np.sin(angle)], axis=0))
    return np.stack(tables).astype(np.float32).astype(bf16)


def lane_tables():
    digit = np.arange(LANES)
    angle = (digit[:, None] * digit[None, :]) % LANES * (2.0 * math.pi / LANES)
    cos_m, sin_m = np.cos(angle), np.sin(angle)
    high, low = split_np(np.block([[cos_m, -sin_m], [sin_m, cos_m]]))
    return np.concatenate([high, low], axis=1)


def twiddle_tables():
    angle = np.arange(ROWS)[:, None] * np.arange(LANES)[None, :] * (2.0 * math.pi / PULSES)
    angle = np.repeat(angle, RB_DEV, axis=0)
    return np.concatenate([np.cos(angle), np.sin(angle)], axis=1).astype(np.float32)


def dot(left, right):
    return jnp.dot(left, right, preferred_element_type=f32)


def split(values):
    high = values.astype(bf16)
    return high, (values - high.astype(f32)).astype(bf16)


def lane_index(shape):
    return lax.broadcasted_iota(jnp.int32, shape, 1)


def compress_kernel(echo_hbm, table_hbm, out_ref, echo, table, folded, bins, echo_sem, table_sem):
    def echo_copy(part):
        return pltpu.make_async_copy(echo_hbm.at[part, 0], echo.at[part], echo_sem.at[part])

    def table_copy(residue):
        return pltpu.make_async_copy(
            table_hbm.at[residue], table.at[residue], table_sem.at[residue]
        )

    for part in range(2):
        echo_copy(part).start()
    for residue in range(RADIX):
        table_copy(residue).start()
    for part in range(2):
        echo_copy(part).wait()

    def put(residue, part, rows, cols, values):
        high, low = split(values)
        folded[residue, part * 64 + rows : part * 64 + rows + 16, cols] = high
        folded[residue, 128 + part * 64 + rows : 128 + part * 64 + rows + 16, cols] = low

    width = 256
    for rows in range(0, PULSES_DEV, 16):
        for left in range(0, FOLD, width):
            cols = slice(left, left + width)
            pieces = [
                [
                    echo[part, rows : rows + 16, a * FOLD + left : a * FOLD + left + width].astype(f32)
                    for a in range(RADIX)
                ]
                for part in range(2)
            ]
            (re0, re1, re2, re3), (im0, im1, im2, im3) = pieces
            re_s, re_t, im_s, im_t = re0 + re2, re1 + re3, im0 + im2, im1 + im3
            put(0, 0, rows, cols, re_s + re_t)
            put(0, 1, rows, cols, im_s + im_t)
            put(2, 0, rows, cols, re_s - re_t)
            put(2, 1, rows, cols, im_s - im_t)
            re_s, re_t, im_s, im_t = re0 - re2, re1 - re3, im0 - im2, im1 - im3
            put(1, 0, rows, cols, re_s + im_t)
            put(1, 1, rows, cols, im_s - re_t)
            put(3, 0, rows, cols, re_s - im_t)
            put(3, 1, rows, cols, im_s + re_t)

    for residue in range(RADIX):
        table_copy(residue).wait()
    sign = jnp.where(lane_index((128, LANES)) < 64, 1.0, -1.0)
    for residue in range(RADIX):
        sums = lax.dot_general(
            table[residue], folded[residue], (((1,), (1,)), ((), ())), preferred_element_type=f32
        )
        sums = sums[:, :LANES] + sums[:, LANES:]
        comp = sums[:128] + sign * pltpu.roll(sums[128:], 64, 1)
        for h in range(2):
            bins[pl.ds(4 * h + residue, N_PULSE, stride=RB_DEV), :] = comp[
                h * N_PULSE : (h + 1) * N_PULSE
            ]
    own = bins[...].astype(bf16).reshape(N_PULSE, RB_DEV, LANES)
    edge = jnp.zeros((1, RB_DEV, LANES), bf16)
    out_ref[0:1, :, 0:LANES] = edge
    out_ref[1:N_PULSE, :, 0:LANES] = own[: N_PULSE - 1]
    out_ref[:, :, LANES : 2 * LANES] = own
    out_ref[0 : N_PULSE - 1, :, 2 * LANES :] = own[1:]
    out_ref[N_PULSE - 1 :, :, 2 * LANES :] = edge


def compress(echoes, tables):
    whole = pl.BlockSpec(memory_space=pl.ANY)
    return pl.pallas_call(
        compress_kernel,
        in_specs=[whole, whole],
        out_shape=jax.ShapeDtypeStruct((N_PULSE, RB_DEV, 3 * LANES), bf16),
        scratch_shapes=[
            pltpu.VMEM((2, PULSES_DEV, NS), bf16),
            pltpu.VMEM((RADIX, 256, FOLD), bf16),
            pltpu.VMEM((RADIX, 256, FOLD), bf16),
            pltpu.VMEM((NR, LANES), f32),
            pltpu.SemaphoreType.DMA((2,)),
            pltpu.SemaphoreType.DMA((RADIX,)),
        ],
        compiler_params=pltpu.CompilerParams(vmem_limit_bytes=60 << 20),
        cost_estimate=pl.CostEstimate(
            flops=2 * RADIX * 256 * 256 * FOLD, bytes_accessed=4 << 20, transcendentals=0
        ),
        name="compress",
    )(echoes, tables)


def add(u, v):
    return (u[0] + v[0], u[1] + v[1])


def sub(u, v):
    return (u[0] - v[0], u[1] - v[1])


def times_i(u):
    return (-u[1], u[0])


def turn(u, angle):
    cos_a, sin_a = math.cos(angle), math.sin(angle)
    return (u[0] * cos_a - u[1] * sin_a, u[1] * cos_a + u[0] * sin_a)


def fft4(v0, v1, v2, v3):
    e0, e1 = add(v0, v2), sub(v0, v2)
    o0, o1 = add(v1, v3), times_i(sub(v1, v3))
    return [add(e0, o0), add(e1, o1), sub(e0, o0), sub(e1, o1)]


def fft8(values):
    half = math.sqrt(0.5)
    even = fft4(values[0], values[2], values[4], values[6])
    odd = fft4(values[1], values[3], values[5], values[7])
    odd[1] = ((odd[1][0] - odd[1][1]) * half, (odd[1][0] + odd[1][1]) * half)
    odd[2] = times_i(odd[2])
    odd[3] = ((-odd[3][0] - odd[3][1]) * half, (odd[3][0] - odd[3][1]) * half)
    return [add(e, o) for e, o in zip(even, odd)] + [sub(e, o) for e, o in zip(even, odd)]


def fft32(load, hold, store):
    for v in range(4):
        firsts = fft8([load(4 * u + v) for u in range(8)])
        for t in range(8):
            value = firsts[t]
            if t * v:
                value = turn(value, 2.0 * math.pi * t * v / 32)
            hold[0, v * 8 + t] = value[0]
            hold[1, v * 8 + t] = value[1]
    for t in range(8):
        seconds = fft4(*[(hold[0, v * 8 + t], hold[1, v * 8 + t]) for v in range(4)])
        for s in range(4):
            store(8 * s + t, seconds[s])


def spectra_kernel(turned_ref, lanes_ref, twiddle_ref, out_ref, hold, samples):
    low_half = lane_index((RB_DEV, LANES)) < 64
    table_hi, table_lo = lanes_ref[:, :256], lanes_ref[:, 256:]
    for group in range(3):
        cols = slice(group * LANES, (group + 1) * LANES)

        def load(p_hi):
            even = turned_ref[2 * p_hi, :, cols].astype(f32)
            odd = turned_ref[2 * p_hi + 1, :, cols].astype(f32)
            real_x = jnp.where(low_half, even, pltpu.roll(odd, 64, 1))
            imag_x = jnp.where(low_half, pltpu.roll(even, 64, 1), odd)
            return (imag_x, real_x)

        def store(j_lo, value):
            imag_y, real_y = value
            rows = slice(j_lo * RB_DEV, (j_lo + 1) * RB_DEV)
            tw_re = twiddle_ref[group, rows, :LANES]
            tw_im = twiddle_ref[group, rows, LANES:]
            samples[group, rows, :LANES] = real_y * tw_re - imag_y * tw_im
            samples[group, rows, LANES:] = imag_y * tw_re + real_y * tw_im

        fft32(load, hold.at[group], store)
        high, low = split(samples[group])
        result = dot(high, table_hi) + (dot(low, table_hi) + dot(high, table_lo))
        out_ref[:, group * 32 : (group + 1) * 32, :] = result.astype(bf16).reshape(
            CHANS, 32, 256
        )


def spectra(turned, lanes_table, twiddle):
    return pl.pallas_call(
        spectra_kernel,
        out_shape=jax.ShapeDtypeStruct((CHANS, 96, 256), bf16),
        scratch_shapes=[
            pltpu.VMEM((3, 2, ROWS, RB_DEV, LANES), f32),
            pltpu.VMEM((3, 256, 256), f32),
        ],
        compiler_params=pltpu.CompilerParams(vmem_limit_bytes=32 << 20),
        cost_estimate=pl.CostEstimate(
            flops=6 * 256 * 256 * 768, bytes_accessed=2 << 20, transcendentals=0
        ),
        name="spectra",
    )(turned, lanes_table, twiddle)


def prepare_kernel(
    scalars,
    rate_ref,
    gain_ref,
    turns_ref,
    filter_ref,
    filt_ref,
    cos_ref,
    sin_ref,
    base_ref,
    lanes_ref,
    twiddle_ref,
    first_ref,
):
    chan = scalars[CHANS]
    block = scalars[CHANS + 1]
    tw_cos = turns_ref[:, :LANES].reshape(ROWS, RB_DEV, LANES)
    tw_sin = turns_ref[:, LANES:].reshape(ROWS, RB_DEV, LANES)
    for group in range(3):
        gain_re, gain_im = gain_ref[0, group][None], gain_ref[1, group][None]
        first_ref[group, :, :LANES] = (gain_re * tw_cos + gain_im * tw_sin).reshape(256, LANES)
        first_ref[group, :, LANES:] = (gain_im * tw_cos - gain_re * tw_sin).reshape(256, LANES)
    shape = (OWN * RB_DEV, LANES)
    row = lax.broadcasted_iota(jnp.int32, shape, 0)
    lane = lax.broadcasted_iota(jnp.int32, shape, 1)
    doppler_bin = 32 * lane + OWN * chan + lax.shift_right_logical(row, 3)
    q = jnp.bitwise_and(row, 7)
    bins = (block * RB_DEV + q).astype(f32)
    slope = 0.5 + 0.5 * bins / NR
    place = (RB_DEV + q).astype(f32)
    rates = jnp.concatenate([rate_ref[...]] * OWN, axis=0)
    for k in range(CHANS):
        doppler = (k * PULSES + doppler_bin).astype(f32) / SPECTRUM - 0.5
        spread = 2.0 * jnp.square(2.0 * doppler) * slope - 1.0
        base_ref[k] = place - (place + MIGRATION * spread)
        phase = -curvature * jnp.square(doppler) / rates
        cos_ref[k] = jnp.cos(phase)
        sin_ref[k] = jnp.sin(phase)
    pick_x = lax.broadcasted_iota(jnp.int32, (1024, LANES), 0)
    pick_y = lax.broadcasted_iota(jnp.int32, (1024, LANES), 1)
    wanted = 32 * jnp.bitwise_and(pick_y, 31) + OWN * chan + lax.shift_right_logical(pick_y, 5)
    pick = jnp.where(pick_x == wanted, 1.0, 0.0).astype(bf16)
    quarter = lax.shift_right_logical(lane_index((128, LANES)), 5)
    picked = [dot(filter_ref[:, 1024 * t : 1024 * (t + 1)], pick) for t in range(4)]
    for digit in range(OWN):
        total = jnp.zeros((128, LANES), f32)
        for t in range(4):
            moved = picked[t]
            if t != digit:
                moved = pltpu.roll(moved, (32 * (t - digit)) % LANES, 1)
            total = jnp.where(quarter == t, moved, total)
        filt_ref[digit] = total
    square = (LANES, LANES)
    j_hi = lax.broadcasted_iota(jnp.int32, square, 0)
    m_lo = lax.broadcasted_iota(jnp.int32, square, 1)
    turns = jnp.bitwise_and(8 * j_hi * m_lo + j_hi * chan, 1023)
    angle = turns.astype(f32) * (2.0 * math.pi / 1024)
    cos_hi, cos_lo = split(jnp.cos(angle))
    sin_hi, sin_lo = split(jnp.sin(angle))
    for at, (cos_m, sin_m) in enumerate(((cos_hi, sin_hi), (cos_lo, sin_lo))):
        left, mid, right = 256 * at, 256 * at + LANES, 256 * at + 256
        lanes_ref[:LANES, left:mid] = cos_m
        lanes_ref[:LANES, mid:right] = sin_m
        lanes_ref[LANES:, left:mid] = -sin_m
        lanes_ref[LANES:, mid:right] = cos_m
    small = (ROWS, LANES)
    j_lo = lax.broadcasted_iota(jnp.int32, small, 0)
    m_low = lax.broadcasted_iota(jnp.int32, small, 1)
    angle = (j_lo * (8 * m_low + chan)).astype(f32) * (2.0 * math.pi / SPECTRUM)
    scale = 1.0 / math.sqrt(SPECTRUM)
    for at, values in enumerate((jnp.cos(angle) * scale, jnp.sin(angle) * scale)):
        full = jnp.broadcast_to(values[:, None, :], (ROWS, RB_DEV, LANES)).reshape(256, LANES)
        twiddle_ref[:, at * LANES : (at + 1) * LANES] = full


def prepare(scalars, rates, gain, turns, filters):
    vmem = pl.BlockSpec(memory_space=pltpu.VMEM)
    return pl.pallas_call(
        prepare_kernel,
        in_specs=[pl.BlockSpec(memory_space=pltpu.SMEM)] + [vmem] * 4,
        out_shape=(
            jax.ShapeDtypeStruct((OWN, 128, LANES), f32),
            jax.ShapeDtypeStruct((CHANS, OWN * RB_DEV, LANES), f32),
            jax.ShapeDtypeStruct((CHANS, OWN * RB_DEV, LANES), f32),
            jax.ShapeDtypeStruct((CHANS, OWN * RB_DEV, LANES), f32),
            jax.ShapeDtypeStruct((256, 512), bf16),
            jax.ShapeDtypeStruct((256, 256), f32),
            jax.ShapeDtypeStruct((3, 256, 256), f32),
        ),
        compiler_params=pltpu.CompilerParams(vmem_limit_bytes=32 << 20),
        cost_estimate=pl.CostEstimate(
            flops=1 << 29, bytes_accessed=2 << 20, transcendentals=1 << 18
        ),
        name="prepare",
    )(scalars, rates, gain, turns, filters)


def band_steps(band):
    doppler = (band * PULSES + np.arange(PULSES)) / SPECTRUM - 0.5
    square = np.square(2.0 * doppler)
    lowest = MIGRATION * (2.0 * square.min() * 0.5 - 1.0) - 1e-3
    highest = MIGRATION * (2.0 * square.max() * (0.5 + 0.5 * (NR - 1) / NR) - 1.0) + 1e-3
    return range(max(-MIGRATION, math.floor(lowest)), min(MIGRATION, math.ceil(highest)) + 1)


def merge_kernel(
    scalars, gathered_ref, filt_ref, cos_ref, sin_ref, base_ref, out_ref, wide, merged, bands
):
    wide[...] = gathered_ref[...].astype(f32)
    for band in range(CHANS):
        steps = band_steps(band)
        groups = [1]
        if steps[0] < 0:
            groups = [0] + groups
        if steps[-1] > 0:
            groups = groups + [2]
        first_row = pl.multiple_of(scalars[CHANS + 2 + band] * 16, 16)
        for digit in range(OWN):
            rows = slice(digit * RB_DEV, (digit + 1) * RB_DEV)
            filters = filt_ref[digit, pl.ds(first_row, 16), :]
            sums_re = [None] * 3
            sums_im = [None] * 3
            for c in range(CHANS):
                f_re = jnp.broadcast_to(filters[2 * c : 2 * c + 1], (RB_DEV, LANES))
                f_im = jnp.broadcast_to(filters[2 * c + 1 : 2 * c + 2], (RB_DEV, LANES))
                for group in groups:
                    at = group * 32 + digit * RB_DEV
                    s_re = wide[c, at : at + RB_DEV, :LANES]
                    s_im = wide[c, at : at + RB_DEV, LANES:]
                    part_re = f_re * s_re - f_im * s_im
                    part_im = f_re * s_im + f_im * s_re
                    sums_re[group] = part_re if c == 0 else sums_re[group] + part_re
                    sums_im[group] = part_im if c == 0 else sums_im[group] + part_im
            slot = (band % 2) * OWN + digit
            for group in groups:
                span = slice(group * RB_DEV, (group + 1) * RB_DEV)
                merged[slot, 0, span, :] = sums_re[group]
                merged[slot, 1, span, :] = sums_im[group]
            base = base_ref[band, rows, :]
            moved_re = moved_im = None
            for step in steps:
                weight = jnp.maximum(0.0, 1.0 - jnp.abs(base + float(step)))
                first = RB_DEV + step
                part_re = weight * merged[slot, 0, first : first + RB_DEV, :]
                part_im = weight * merged[slot, 1, first : first + RB_DEV, :]
                moved_re = part_re if moved_re is None else moved_re + part_re
                moved_im = part_im if moved_im is None else moved_im + part_im
            cos_p = cos_ref[band, rows, :]
            sin_p = sin_ref[band, rows, :]
            bands[band, 0, rows, :] = moved_re * cos_p - moved_im * sin_p
            bands[band, 1, rows, :] = moved_im * cos_p + moved_re * sin_p
    for half in range(OWN * RB_DEV // 16):
        rows = slice(half * 16, half * 16 + 16)
        results = fft8([(bands[k, 0, rows, :], bands[k, 1, rows, :]) for k in range(CHANS)])
        for a in range(CHANS):
            out_ref[a, rows, :LANES] = results[a][0].astype(bf16)
            out_ref[a, rows, LANES:] = results[a][1].astype(bf16)


def merge(scalars, gathered, filt, cos_p, sin_p, base):
    vmem = pl.BlockSpec(memory_space=pltpu.VMEM)
    return pl.pallas_call(
        merge_kernel,
        in_specs=[pl.BlockSpec(memory_space=pltpu.SMEM)] + [vmem] * 5,
        out_shape=jax.ShapeDtypeStruct((CHANS, OWN * RB_DEV, 256), bf16),
        scratch_shapes=[
            pltpu.VMEM((CHANS, 96, 256), f32),
            pltpu.VMEM((2 * OWN, 2, 3 * RB_DEV, LANES), f32),
            pltpu.VMEM((CHANS, 2, OWN * RB_DEV, LANES), f32),
        ],
        compiler_params=pltpu.CompilerParams(vmem_limit_bytes=32 << 20),
        cost_estimate=pl.CostEstimate(flops=1 << 24, bytes_accessed=2 << 20, transcendentals=0),
        name="merge",
    )(scalars, gathered, filt, cos_p, sin_p, base)


def image_kernel(combined_ref, lanes_ref, twiddle_ref, out_ref, hold, samples):
    turned = dot(combined_ref[...].reshape(256, 256), lanes_ref[...])
    samples[...] = turned[:, :256] + turned[:, 256:]

    def load(j_lo):
        rows = slice(j_lo * RB_DEV, (j_lo + 1) * RB_DEV)
        real_y, imag_y = samples[rows, :LANES], samples[rows, LANES:]
        tw_cos, tw_sin = twiddle_ref[rows, :LANES], twiddle_ref[rows, LANES:]
        return (real_y * tw_cos - imag_y * tw_sin, imag_y * tw_cos + real_y * tw_sin)

    def store(m_hi, value):
        cols = slice(m_hi * LANES, (m_hi + 1) * LANES)
        out_ref[0, :, cols] = value[0]
        out_ref[1, :, cols] = value[1]

    fft32(load, hold, store)


def image(combined, lanes_table, twiddle):
    return pl.pallas_call(
        image_kernel,
        out_shape=jax.ShapeDtypeStruct((2, RB_DEV, PULSES), f32),
        scratch_shapes=[
            pltpu.VMEM((2, ROWS, RB_DEV, LANES), f32),
            pltpu.VMEM((256, 256), f32),
        ],
        compiler_params=pltpu.CompilerParams(vmem_limit_bytes=32 << 20),
        cost_estimate=pl.CostEstimate(
            flops=2 * 256 * 256 * 512, bytes_accessed=2 << 20, transcendentals=0
        ),
        name="image",
    )(combined, lanes_table, twiddle)


def window_gain(range_phase, band_lo, band_hi, block_index):
    slab_bins = block_index * RB_DEV - RB_DEV + lax.iota(jnp.int32, 3 * RB_DEV)
    inside = (slab_bins >= band_lo[0]) & (slab_bins < band_hi[0])
    scale = jnp.where(inside, 1.0 / math.sqrt(NS * PULSES), 0.0)
    phase = lax.dynamic_slice(
        jnp.pad(range_phase, (RB_DEV, RB_DEV)), (block_index * RB_DEV,), (3 * RB_DEV,)
    )
    gain = jnp.stack([scale * jnp.cos(phase), scale * jnp.sin(phase)])
    return jnp.broadcast_to(gain.reshape(2, 3, RB_DEV, 1), (2, 3, RB_DEV, LANES))


def per_device(echoes, range_phase, azimuth_rate, band_lo, band_hi, band_map, recon_filter):
    block_index = lax.axis_index("pulse").astype(jnp.int32)
    own_index = lax.axis_index("chan").astype(jnp.int32)
    order = lax.iota(jnp.int32, CHANS)
    row_of_band = jnp.sum(
        jnp.where(band_map[None, :] == order[:, None], order[None, :], 0), axis=1
    )
    scalars = jnp.concatenate([band_map, jnp.stack([own_index, block_index]), row_of_band])
    windows = compress(echoes, jnp.asarray(range_tables()))
    turned = lax.all_to_all(windows, "pulse", split_axis=0, concat_axis=0, tiled=True)
    gain = window_gain(range_phase, band_lo, band_hi, block_index)
    rates = jnp.broadcast_to(azimuth_rate[:, None], (RB_DEV, LANES))
    filt, cos_p, sin_p, base, last_lanes, last_twiddle, first_twiddle = prepare(
        scalars,
        rates,
        gain,
        jnp.asarray(twiddle_tables()),
        recon_filter.reshape(2 * CHANS * CHANS, PULSES),
    )
    doppler = spectra(turned, jnp.asarray(lane_tables()), first_twiddle)
    gathered = lax.all_to_all(doppler, "chan", split_axis=0, concat_axis=0, tiled=True)
    summed = merge(scalars, gathered, filt, cos_p, sin_p, base)
    combined = lax.all_to_all(summed, "chan", split_axis=0, concat_axis=0, tiled=True)
    return image(combined, last_lanes, last_twiddle)


def solution(mesh):
    in_specs = (P(None, "chan", "pulse", None), P(), P("pulse"), P("pulse"), P("pulse"), P(), P())
    out_specs = P(None, "pulse", "chan")
    return jax.shard_map(
        per_device, mesh=mesh, in_specs=in_specs, out_specs=out_specs, check_vma=False
    )
```

```python
import math

import jax
import jax.numpy as jnp
import numpy as np
from jax import lax
from jax.experimental import pallas as pl
from jax.experimental.pallas import tpu as pltpu
from jax.sharding import PartitionSpec as P

NS = 4096
RB_DEV = 8
MIGRATION = 7
PULSES = 4096
NR = 512
CHANS = 8
SPECTRUM = 32768
N_PULSE = 64

RADIX = 4
FOLD = NS // RADIX
LANES = 128
ROWS = PULSES // LANES
PAIR = 2
OWN = ROWS // (PAIR * CHANS)
OUT_ROWS = PAIR * RB_DEV * OWN
PULSES_DEV = PULSES // N_PULSE
curvature = 300.0

f32 = jnp.float32
bf16 = jnp.bfloat16


def split_np(values):
    high = np.asarray(values, np.float32).astype(bf16)
    low = (values - high.astype(np.float64)).astype(np.float32).astype(bf16)
    return high, low


def range_tables():
    tables = []
    sample = np.arange(FOLD)
    for rho in range(RADIX):
        bins = np.array([8 * block + 4 * h + rho for h in range(2) for block in range(N_PULSE)])
        angle = (bins[:, None] * sample[None, :]) % NS * (2.0 * math.pi / NS)
        tables.append(np.concatenate([np.cos(angle), np.sin(angle)], axis=0))
    return np.stack(tables).astype(np.float32).astype(bf16)


def lane_tables():
    digit = np.arange(LANES)
    angle = (digit[:, None] * digit[None, :]) % LANES * (2.0 * math.pi / LANES)
    cos_m, sin_m = np.cos(angle), np.sin(angle)
    high, low = split_np(np.block([[cos_m, -sin_m], [sin_m, cos_m]]))
    return np.concatenate([high, low], axis=1)


def twiddle_tables():
    angle = np.arange(ROWS)[:, None] * np.arange(LANES)[None, :] * (2.0 * math.pi / PULSES)
    angle = np.repeat(angle, RB_DEV, axis=0)
    return np.concatenate([np.cos(angle), np.sin(angle)], axis=1).astype(np.float32)


def dot(left, right):
    return jnp.dot(left, right, preferred_element_type=f32)


def split(values):
    high = values.astype(bf16)
    return high, (values - high.astype(f32)).astype(bf16)


def lane_index(shape):
    return lax.broadcasted_iota(jnp.int32, shape, 1)


def compress_kernel(
    echo_hbm,
    table_hbm,
    out_ref,
    zero_ref,
    echo,
    table,
    folded,
    bins,
    echo_sem,
    table_sem,
):
    def echo_copy(part):
        return pltpu.make_async_copy(echo_hbm.at[part, 0], echo.at[part], echo_sem.at[part])

    def table_copy(residue):
        return pltpu.make_async_copy(
            table_hbm.at[residue], table.at[residue], table_sem.at[residue]
        )

    for part in range(2):
        echo_copy(part).start()
    for residue in range(RADIX):
        table_copy(residue).start()
    for part in range(2):
        echo_copy(part).wait()

    def put(residue, part, rows, cols, values):
        high, low = split(values)
        folded[residue, part * 64 + rows : part * 64 + rows + 16, cols] = high
        folded[residue, 128 + part * 64 + rows : 128 + part * 64 + rows + 16, cols] = low

    width = 256
    for rows in range(0, PULSES_DEV, 16):
        for left in range(0, FOLD, width):
            cols = slice(left, left + width)
            pieces = [
                [
                    echo[part, rows : rows + 16, a * FOLD + left : a * FOLD + left + width].astype(f32)
                    for a in range(RADIX)
                ]
                for part in range(2)
            ]
            (re0, re1, re2, re3), (im0, im1, im2, im3) = pieces
            re_s, re_t, im_s, im_t = re0 + re2, re1 + re3, im0 + im2, im1 + im3
            put(0, 0, rows, cols, re_s + re_t)
            put(0, 1, rows, cols, im_s + im_t)
            put(2, 0, rows, cols, re_s - re_t)
            put(2, 1, rows, cols, im_s - im_t)
            re_s, re_t, im_s, im_t = re0 - re2, re1 - re3, im0 - im2, im1 - im3
            put(1, 0, rows, cols, re_s + im_t)
            put(1, 1, rows, cols, im_s - re_t)
            put(3, 0, rows, cols, re_s - im_t)
            put(3, 1, rows, cols, im_s + re_t)

    for residue in range(RADIX):
        table_copy(residue).wait()
    zero_ref[...] = jnp.zeros((RB_DEV, LANES), f32)
    sign = jnp.where(lane_index((128, LANES)) < 64, 1.0, -1.0)
    for residue in range(RADIX):
        sums = lax.dot_general(
            table[residue], folded[residue], (((1,), (1,)), ((), ())), preferred_element_type=f32
        )
        sums = sums[:, :LANES] + sums[:, LANES:]
        comp = sums[:128] + sign * pltpu.roll(sums[128:], 64, 1)
        for h in range(2):
            bins[pl.ds(4 * h + residue, N_PULSE, stride=RB_DEV), :] = comp[
                h * N_PULSE : (h + 1) * N_PULSE
            ]
    own = bins[...].astype(bf16).reshape(N_PULSE // 2, 2, RB_DEV, LANES)
    even, odd = own[:, 0], own[:, 1]
    edge = jnp.zeros((1, RB_DEV, LANES), bf16)
    last = N_PULSE // 2 - 1
    out_ref[0:1, 0, :, :LANES] = edge
    out_ref[1:, 0, :, :LANES] = odd[:last]
    out_ref[:, 0, :, LANES:] = even
    out_ref[:, 1, :, :LANES] = odd
    out_ref[:last, 1, :, LANES:] = even[1:]
    out_ref[last:, 1, :, LANES:] = edge


def compress(echoes, tables):
    windows, zeros = pl.pallas_call(
        compress_kernel,
        in_specs=[pl.BlockSpec(memory_space=pl.ANY)] * 2,
        out_shape=(
            jax.ShapeDtypeStruct((N_PULSE // 2, 2, RB_DEV, 2 * LANES), bf16),
            jax.ShapeDtypeStruct((RB_DEV, LANES), f32),
        ),
        scratch_shapes=[
            pltpu.VMEM((2, PULSES_DEV, NS), bf16),
            pltpu.VMEM((RADIX, 256, FOLD), bf16),
            pltpu.VMEM((RADIX, 256, FOLD), bf16),
            pltpu.VMEM((NR, LANES), f32),
            pltpu.SemaphoreType.DMA((2,)),
            pltpu.SemaphoreType.DMA((RADIX,)),
        ],
        compiler_params=pltpu.CompilerParams(vmem_limit_bytes=60 << 20),
        cost_estimate=pl.CostEstimate(
            flops=2 * RADIX * 256 * 256 * FOLD, bytes_accessed=4 << 20, transcendentals=0
        ),
        name="compress",
    )(echoes, tables)
    return windows.reshape(N_PULSE, RB_DEV, 2 * LANES), zeros


def add(u, v):
    return (u[0] + v[0], u[1] + v[1])


def sub(u, v):
    return (u[0] - v[0], u[1] - v[1])


def times_i(u):
    return (-u[1], u[0])


def turn(u, angle):
    cos_a, sin_a = math.cos(angle), math.sin(angle)
    return (u[0] * cos_a - u[1] * sin_a, u[1] * cos_a + u[0] * sin_a)


def fft4(v0, v1, v2, v3):
    e0, e1 = add(v0, v2), sub(v0, v2)
    o0, o1 = add(v1, v3), times_i(sub(v1, v3))
    return [add(e0, o0), add(e1, o1), sub(e0, o0), sub(e1, o1)]


def fft8(values):
    half = math.sqrt(0.5)
    even = fft4(values[0], values[2], values[4], values[6])
    odd = fft4(values[1], values[3], values[5], values[7])
    odd[1] = ((odd[1][0] - odd[1][1]) * half, (odd[1][0] + odd[1][1]) * half)
    odd[2] = times_i(odd[2])
    odd[3] = ((-odd[3][0] - odd[3][1]) * half, (odd[3][0] - odd[3][1]) * half)
    return [add(e, o) for e, o in zip(even, odd)] + [sub(e, o) for e, o in zip(even, odd)]


def fft32(load, hold, store):
    for v in range(4):
        firsts = fft8([load(4 * u + v) for u in range(8)])
        for t in range(8):
            value = firsts[t]
            if t * v:
                value = turn(value, 2.0 * math.pi * t * v / 32)
            hold[0, v * 8 + t] = value[0]
            hold[1, v * 8 + t] = value[1]
    for t in range(8):
        seconds = fft4(*[(hold[0, v * 8 + t], hold[1, v * 8 + t]) for v in range(4)])
        for s in range(4):
            store(8 * s + t, seconds[s])


def spectra_kernel(turned_ref, lanes_ref, twiddle_ref, after_ref, out_ref, hold, samples):
    del after_ref
    low_half = lane_index((RB_DEV, LANES)) < 64
    table_hi, table_lo = lanes_ref[:, :256], lanes_ref[:, 256:]
    for group in range(2):
        cols = slice(group * LANES, (group + 1) * LANES)

        def load(p_hi):
            even = turned_ref[2 * p_hi, :, cols].astype(f32)
            odd = turned_ref[2 * p_hi + 1, :, cols].astype(f32)
            real_x = jnp.where(low_half, even, pltpu.roll(odd, 64, 1))
            imag_x = jnp.where(low_half, pltpu.roll(even, 64, 1), odd)
            return (imag_x, real_x)

        def store(j_lo, value):
            imag_y, real_y = value
            rows = slice(j_lo * RB_DEV, (j_lo + 1) * RB_DEV)
            tw_re = twiddle_ref[group, rows, :LANES]
            tw_im = twiddle_ref[group, rows, LANES:]
            samples[group, rows, :LANES] = real_y * tw_re - imag_y * tw_im
            samples[group, rows, LANES:] = imag_y * tw_re + real_y * tw_im

        fft32(load, hold.at[group], store)
        high, low = split(samples[group])
        result = dot(high, table_hi) + (dot(low, table_hi) + dot(high, table_lo))
        out_ref[:, group * 16 : (group + 1) * 16, :] = result.astype(bf16).reshape(
            PAIR * CHANS, 16, 256
        )


def spectra(turned, lanes_table, twiddle, after):
    vmem = pl.BlockSpec(memory_space=pltpu.VMEM)
    return pl.pallas_call(
        spectra_kernel,
        in_specs=[vmem] * 3 + [pl.BlockSpec(memory_space=pl.ANY)],
        out_shape=jax.ShapeDtypeStruct((PAIR * CHANS, 32, 256), bf16),
        scratch_shapes=[
            pltpu.VMEM((2, 2, ROWS, RB_DEV, LANES), f32),
            pltpu.VMEM((2, 256, 256), f32),
        ],
        compiler_params=pltpu.CompilerParams(vmem_limit_bytes=32 << 20),
        cost_estimate=pl.CostEstimate(
            flops=4 * 256 * 256 * 768, bytes_accessed=2 << 20, transcendentals=0
        ),
        name="spectra",
    )(turned, lanes_table, twiddle, after)


def doppler_rows(scalars):
    block = scalars[CHANS + 1]
    member = jnp.bitwise_and(block, 1)
    shape = (OUT_ROWS, LANES)
    row = lax.broadcasted_iota(jnp.int32, shape, 0)
    lane = lax.broadcasted_iota(jnp.int32, shape, 1)
    digit = OWN * (member * CHANS + scalars[CHANS]) + lax.shift_right_logical(row, 4)
    bins = (block - member) * RB_DEV + jnp.bitwise_and(row, 15)
    return 32 * lane + digit, bins.astype(f32), jnp.bitwise_and(row, 7).astype(f32)


def doppler_of(band, doppler_bin):
    return (band * PULSES + doppler_bin).astype(f32) / SPECTRUM - 0.5


def tables_kernel(
    scalars,
    gain_ref,
    turns_ref,
    filter_ref,
    filt_ref,
    lanes_ref,
    twiddle_ref,
    base_ref,
    first_ref,
):
    chan = scalars[CHANS]
    first_digit = OWN * (jnp.bitwise_and(scalars[CHANS + 1], 1) * CHANS + chan)
    tw_cos = turns_ref[:, :LANES].reshape(ROWS, RB_DEV, LANES)
    tw_sin = turns_ref[:, LANES:].reshape(ROWS, RB_DEV, LANES)
    for group in range(2):
        gain_re, gain_im = gain_ref[0, group][None], gain_ref[1, group][None]
        first_ref[group, :, :LANES] = (gain_re * tw_cos + gain_im * tw_sin).reshape(256, LANES)
        first_ref[group, :, LANES:] = (gain_im * tw_cos - gain_re * tw_sin).reshape(256, LANES)
    doppler_bin, bins, q = doppler_rows(scalars)
    slope = 0.5 + 0.5 * bins / NR
    place = RB_DEV + q
    for k in range(CHANS):
        spread = 2.0 * jnp.square(2.0 * doppler_of(k, doppler_bin)) * slope - 1.0
        base_ref[k] = place - (place + MIGRATION * spread)
    pick_x = lax.broadcasted_iota(jnp.int32, (2048, LANES), 0)
    pick_y = lax.broadcasted_iota(jnp.int32, (2048, LANES), 1)
    wanted = 32 * jnp.bitwise_and(pick_y, 63) + first_digit + lax.shift_right_logical(pick_y, 6)
    pick = jnp.where(pick_x == wanted, 1.0, 0.0).astype(bf16)
    low_half = lane_index((128, LANES)) < 64
    left, right = [dot(filter_ref[:, 2048 * t : 2048 * (t + 1)], pick) for t in range(2)]
    filt_ref[0] = jnp.where(low_half, left, pltpu.roll(right, 64, 1))
    filt_ref[1] = jnp.where(low_half, pltpu.roll(left, 64, 1), right)
    square = (LANES, LANES)
    j_hi = lax.broadcasted_iota(jnp.int32, square, 0)
    m_lo = lax.broadcasted_iota(jnp.int32, square, 1)
    turns = jnp.bitwise_and(8 * j_hi * m_lo + j_hi * chan, 1023)
    angle = turns.astype(f32) * (2.0 * math.pi / 1024)
    cos_hi, cos_lo = split(jnp.cos(angle))
    sin_hi, sin_lo = split(jnp.sin(angle))
    for at, (cos_m, sin_m) in enumerate(((cos_hi, sin_hi), (cos_lo, sin_lo))):
        left, mid, right = 256 * at, 256 * at + LANES, 256 * at + 256
        lanes_ref[:LANES, left:mid] = cos_m
        lanes_ref[:LANES, mid:right] = sin_m
        lanes_ref[LANES:, left:mid] = -sin_m
        lanes_ref[LANES:, mid:right] = cos_m
    small = (ROWS, LANES)
    j_lo = lax.broadcasted_iota(jnp.int32, small, 0)
    m_low = lax.broadcasted_iota(jnp.int32, small, 1)
    angle = (j_lo * (8 * m_low + chan)).astype(f32) * (2.0 * math.pi / SPECTRUM)
    scale = 1.0 / math.sqrt(SPECTRUM)
    for at, values in enumerate((jnp.cos(angle) * scale, jnp.sin(angle) * scale)):
        full = jnp.broadcast_to(values[:, None, :], (ROWS, RB_DEV, LANES)).reshape(256, LANES)
        twiddle_ref[:, at * LANES : (at + 1) * LANES] = full


def tables(scalars, gain, turns, filters):
    vmem = pl.BlockSpec(memory_space=pltpu.VMEM)
    return pl.pallas_call(
        tables_kernel,
        in_specs=[pl.BlockSpec(memory_space=pltpu.SMEM)] + [vmem] * 3,
        out_shape=(
            jax.ShapeDtypeStruct((OWN, 128, LANES), f32),
            jax.ShapeDtypeStruct((256, 512), bf16),
            jax.ShapeDtypeStruct((256, 256), f32),
            jax.ShapeDtypeStruct((CHANS, OUT_ROWS, LANES), f32),
            jax.ShapeDtypeStruct((2, 256, 256), f32),
        ),
        compiler_params=pltpu.CompilerParams(vmem_limit_bytes=32 << 20),
        cost_estimate=pl.CostEstimate(
            flops=1 << 28, bytes_accessed=2 << 20, transcendentals=1 << 16
        ),
        name="tables",
    )(scalars, gain, turns, filters)


def phases_kernel(scalars, own_ref, other_ref, cos_ref, sin_ref, mask_ref):
    block = scalars[CHANS + 1]
    member = jnp.bitwise_and(block, 1)
    pair_start = (block - member) * RB_DEV
    own, other = own_ref[...], other_ref[...]
    given = [jnp.where(member == h, own, other) for h in range(PAIR)]
    shape = (RB_DEV, LANES)
    row = lax.broadcasted_iota(jnp.int32, shape, 0)
    for h in range(PAIR):
        low = jnp.broadcast_to(given[h][:, 64:65], shape)
        high = jnp.broadcast_to(given[h][:, 96:97], shape)
        for group in range(3):
            bins = (pair_start + (h + group - 1) * RB_DEV + row).astype(f32)
            inside = jnp.where(bins >= low, 1.0, 0.0) * jnp.where(bins < high, 1.0, 0.0)
            mask_ref[h, group] = inside
    doppler_bin = doppler_rows(scalars)[0]
    rates = [jnp.broadcast_to(given[h][:, 0:1], (RB_DEV, LANES)) for h in range(PAIR)]
    rates = jnp.concatenate(rates * OWN, axis=0)
    for k in range(CHANS):
        phase = -curvature * jnp.square(doppler_of(k, doppler_bin)) / rates
        cos_ref[k] = jnp.cos(phase)
        sin_ref[k] = jnp.sin(phase)


def phases(scalars, own, other):
    vmem = pl.BlockSpec(memory_space=pltpu.VMEM)
    rows = jax.ShapeDtypeStruct((CHANS, OUT_ROWS, LANES), f32)
    return pl.pallas_call(
        phases_kernel,
        in_specs=[pl.BlockSpec(memory_space=pltpu.SMEM)] + [vmem] * 2,
        out_shape=(
            rows,
            rows,
            jax.ShapeDtypeStruct((PAIR, 3, RB_DEV, LANES), f32),
        ),
        compiler_params=pltpu.CompilerParams(vmem_limit_bytes=32 << 20),
        cost_estimate=pl.CostEstimate(
            flops=1 << 24, bytes_accessed=1 << 20, transcendentals=1 << 18
        ),
        name="phases",
    )(scalars, own, other)


def band_steps(band):
    doppler = (band * PULSES + np.arange(PULSES)) / SPECTRUM - 0.5
    square = np.square(2.0 * doppler)
    lowest = MIGRATION * (2.0 * square.min() * 0.5 - 1.0) - 1e-3
    highest = MIGRATION * (2.0 * square.max() * (0.5 + 0.5 * (NR - 1) / NR) - 1.0) + 1e-3
    return range(max(-MIGRATION, math.floor(lowest)), min(MIGRATION, math.ceil(highest)) + 1)


def merge_kernel(
    scalars,
    gathered_ref,
    filt_ref,
    cos_ref,
    sin_ref,
    base_ref,
    mask_ref,
    out_ref,
    wide,
    merged,
    bands,
):
    wide[...] = gathered_ref[...].astype(f32)
    for band in range(CHANS):
        steps = band_steps(band)
        reach = [group for group, used in ((0, steps[0] < 0), (1, True), (2, steps[-1] > 0)) if used]
        needed = sorted({h + group for h in range(PAIR) for group in reach})
        first_row = pl.multiple_of(scalars[CHANS + 2 + band] * 16, 16)
        for digit in range(OWN):
            filters = filt_ref[digit, pl.ds(first_row, 16), :]
            sums_re = [None] * 4
            sums_im = [None] * 4
            for c in range(CHANS):
                f_re = jnp.broadcast_to(filters[2 * c : 2 * c + 1], (RB_DEV, LANES))
                f_im = jnp.broadcast_to(filters[2 * c + 1 : 2 * c + 2], (RB_DEV, LANES))
                for part in needed:
                    source = (part // 2) * CHANS + c
                    at = (part % 2) * 16 + digit * RB_DEV
                    s_re = wide[source, at : at + RB_DEV, :LANES]
                    s_im = wide[source, at : at + RB_DEV, LANES:]
                    part_re = f_re * s_re - f_im * s_im
                    part_im = f_re * s_im + f_im * s_re
                    sums_re[part] = part_re if c == 0 else sums_re[part] + part_re
                    sums_im[part] = part_im if c == 0 else sums_im[part] + part_im
            for h in range(PAIR):
                slot = ((band % 2) * OWN + digit) * PAIR + h
                for group in reach:
                    span = slice(group * RB_DEV, (group + 1) * RB_DEV)
                    inside = mask_ref[h, group]
                    merged[slot, 0, span, :] = sums_re[h + group] * inside
                    merged[slot, 1, span, :] = sums_im[h + group] * inside
                at = digit * PAIR * RB_DEV + h * RB_DEV
                rows = slice(at, at + RB_DEV)
                base = base_ref[band, rows, :]
                moved_re = moved_im = None
                for step in steps:
                    weight = jnp.maximum(0.0, 1.0 - jnp.abs(base + float(step)))
                    first = RB_DEV + step
                    part_re = weight * merged[slot, 0, first : first + RB_DEV, :]
                    part_im = weight * merged[slot, 1, first : first + RB_DEV, :]
                    moved_re = part_re if moved_re is None else moved_re + part_re
                    moved_im = part_im if moved_im is None else moved_im + part_im
                cos_p = cos_ref[band, rows, :]
                sin_p = sin_ref[band, rows, :]
                to = slice(digit * RB_DEV, (digit + 1) * RB_DEV)
                bands[band, 0, h, to, :] = moved_re * cos_p - moved_im * sin_p
                bands[band, 1, h, to, :] = moved_im * cos_p + moved_re * sin_p
    for h in range(PAIR):
        results = fft8([(bands[k, 0, h], bands[k, 1, h]) for k in range(CHANS)])
        for a in range(CHANS):
            out_ref[h * CHANS + a, :, :LANES] = results[a][0].astype(bf16)
            out_ref[h * CHANS + a, :, LANES:] = results[a][1].astype(bf16)


def merge(scalars, gathered, filt, cos_p, sin_p, base, mask):
    vmem = pl.BlockSpec(memory_space=pltpu.VMEM)
    return pl.pallas_call(
        merge_kernel,
        in_specs=[pl.BlockSpec(memory_space=pltpu.SMEM)] + [vmem] * 6,
        out_shape=jax.ShapeDtypeStruct((PAIR * CHANS, OWN * RB_DEV, 256), bf16),
        scratch_shapes=[
            pltpu.VMEM((PAIR * CHANS, 32, 256), f32),
            pltpu.VMEM((2 * OWN * PAIR, 2, 3 * RB_DEV, LANES), f32),
            pltpu.VMEM((CHANS, 2, PAIR, OWN * RB_DEV, LANES), f32),
        ],
        compiler_params=pltpu.CompilerParams(vmem_limit_bytes=32 << 20),
        cost_estimate=pl.CostEstimate(flops=1 << 24, bytes_accessed=2 << 20, transcendentals=0),
        name="merge",
    )(scalars, gathered, filt, cos_p, sin_p, base, mask)


def image_kernel(combined_ref, lanes_ref, twiddle_ref, out_ref, hold, samples):
    turned = dot(combined_ref[...].reshape(256, 256), lanes_ref[...])
    samples[...] = turned[:, :256] + turned[:, 256:]

    def load(j_lo):
        rows = slice(j_lo * RB_DEV, (j_lo + 1) * RB_DEV)
        real_y, imag_y = samples[rows, :LANES], samples[rows, LANES:]
        tw_cos, tw_sin = twiddle_ref[rows, :LANES], twiddle_ref[rows, LANES:]
        return (real_y * tw_cos - imag_y * tw_sin, imag_y * tw_cos + real_y * tw_sin)

    def store(m_hi, value):
        cols = slice(m_hi * LANES, (m_hi + 1) * LANES)
        out_ref[0, :, cols] = value[0]
        out_ref[1, :, cols] = value[1]

    fft32(load, hold, store)


def image(combined, lanes_table, twiddle):
    return pl.pallas_call(
        image_kernel,
        out_shape=jax.ShapeDtypeStruct((2, RB_DEV, PULSES), f32),
        scratch_shapes=[
            pltpu.VMEM((2, ROWS, RB_DEV, LANES), f32),
            pltpu.VMEM((256, 256), f32),
        ],
        compiler_params=pltpu.CompilerParams(vmem_limit_bytes=32 << 20),
        cost_estimate=pl.CostEstimate(
            flops=2 * 256 * 256 * 512, bytes_accessed=2 << 20, transcendentals=0
        ),
        name="image",
    )(combined, lanes_table, twiddle)


def window_gain(range_phase, first_bin):
    padded = jnp.pad(range_phase, (RB_DEV, RB_DEV))
    phase = lax.dynamic_slice(padded, (first_bin + RB_DEV,), (2 * RB_DEV,))
    scale = 1.0 / math.sqrt(NS * PULSES)
    gain = jnp.stack([scale * jnp.cos(phase), scale * jnp.sin(phase)])
    return jnp.broadcast_to(gain.reshape(2, 2, RB_DEV, 1), (2, 2, RB_DEV, LANES))


def block_values(azimuth_rate, band_lo, band_hi):
    return jnp.concatenate(
        [
            jnp.broadcast_to(azimuth_rate[:, None], (RB_DEV, 64)),
            jnp.broadcast_to(band_lo.astype(f32)[None, :], (RB_DEV, 32)),
            jnp.broadcast_to(band_hi.astype(f32)[None, :], (RB_DEV, 32)),
        ],
        axis=1,
    )


def per_device(echoes, range_phase, azimuth_rate, band_lo, band_hi, band_map, recon_filter):
    block_index = lax.axis_index("pulse").astype(jnp.int32)
    own_index = lax.axis_index("chan").astype(jnp.int32)
    order = lax.iota(jnp.int32, CHANS)
    row_of_band = jnp.sum(
        jnp.where(band_map[None, :] == order[:, None], order[None, :], 0), axis=1
    )
    scalars = jnp.concatenate([band_map, jnp.stack([own_index, block_index]), row_of_band])
    groups = [
        [(PAIR * i + h) * CHANS + d for h in range(PAIR) for d in range(CHANS)]
        for i in range(N_PULSE // PAIR)
    ]

    def exchange(values):
        return lax.all_to_all(
            values,
            ("pulse", "chan"),
            split_axis=0,
            concat_axis=0,
            axis_index_groups=groups,
            tiled=True,
        )

    windows, zeros = compress(echoes, jnp.asarray(range_tables()))
    turned = lax.all_to_all(windows, "pulse", split_axis=0, concat_axis=0, tiled=True)
    first_bin = (block_index - 1 + jnp.bitwise_and(block_index, 1)) * RB_DEV
    given = zeros + block_values(azimuth_rate, band_lo, band_hi)
    other = lax.ppermute(given, "pulse", [(b, b ^ 1) for b in range(N_PULSE)])
    filt, last_lanes, last_twiddle, base, first_twiddle = tables(
        scalars,
        window_gain(range_phase, first_bin),
        jnp.asarray(twiddle_tables()),
        recon_filter.reshape(2 * CHANS * CHANS, PULSES),
    )
    cos_p, sin_p, mask = phases(scalars, given, other)
    doppler = spectra(turned, jnp.asarray(lane_tables()), first_twiddle, mask)
    gathered = exchange(doppler)
    summed = merge(scalars, gathered, filt, cos_p, sin_p, base, mask)
    combined = exchange(summed)
    return image(combined, last_lanes, last_twiddle)


def solution(mesh):
    in_specs = (P(None, "chan", "pulse", None), P(), P("pulse"), P("pulse"), P("pulse"), P(), P())
    out_specs = P(None, "pulse", "chan")
    return jax.shard_map(
        per_device, mesh=mesh, in_specs=in_specs, out_specs=out_specs, check_vma=False
    )
```

```python
import math

import jax
import jax.numpy as jnp
import numpy as np
from jax import lax
from jax.experimental import pallas as pl
from jax.experimental.pallas import tpu as pltpu
from jax.sharding import PartitionSpec as P

NS = 4096
RB_DEV = 8
MIGRATION = 7
PULSES = 4096
NR = 512
CHANS = 8
SPECTRUM = 32768
N_PULSE = 64

RADIX = 4
FOLD = NS // RADIX
LANES = 128
ROWS = PULSES // LANES
PAIR = 2
LAST = PAIR * CHANS - 1
OWN = ROWS // (PAIR * CHANS)
OUT_ROWS = PAIR * RB_DEV * OWN
PULSES_DEV = PULSES // N_PULSE
STRIP = 32
curvature = 300.0

f32 = jnp.float32
bf16 = jnp.bfloat16


def split_np(values):
    high = np.asarray(values, np.float32).astype(bf16)
    low = (values - high.astype(np.float64)).astype(np.float32).astype(bf16)
    return high, low


def range_table(bins, samples):
    angle = (np.asarray(bins)[:, None] * np.arange(samples)[None, :]) % NS * (2.0 * math.pi / NS)
    table = np.concatenate([np.cos(angle), np.sin(angle)], axis=0)
    return table.astype(np.float32).astype(bf16)


def odd_tables():
    blocks = RB_DEV * np.arange(N_PULSE)[::-1]
    return np.stack(
        [range_table(np.concatenate([blocks + r, blocks + 4 + r]), FOLD) for r in (1, 3)]
    )


def even_tables():
    blocks = RB_DEV * np.arange(N_PULSE)[::-1]
    return np.stack([range_table(blocks + 2 * e, FOLD // 2) for e in range(4)])


def lane_tables():
    digit = np.arange(LANES)
    angle = (digit[:, None] * digit[None, :]) % LANES * (2.0 * math.pi / LANES)
    cos_m, sin_m = np.cos(angle), np.sin(angle)
    high, low = split_np(np.block([[cos_m, -sin_m], [sin_m, cos_m]]))
    return np.concatenate([high, low], axis=1)


def twiddle_tables():
    angle = np.arange(ROWS)[:, None] * np.arange(LANES)[None, :] * (2.0 * math.pi / PULSES)
    angle = np.repeat(angle, RB_DEV, axis=0)
    return np.concatenate([np.cos(angle), np.sin(angle)], axis=1).astype(np.float32)


def dot(left, right):
    return jnp.dot(left, right, preferred_element_type=f32)


def split(values):
    high = values.astype(bf16)
    return high, (values - high.astype(f32)).astype(bf16)


def lane_index(shape):
    return lax.broadcasted_iota(jnp.int32, shape, 1)


def compress_kernel(
    echo_hbm,
    odd_hbm,
    even_hbm,
    out_ref,
    zero_ref,
    echo,
    odd,
    even,
    odd_sums,
    even_sums,
    bins,
    echo_sem,
    table_sem,
):
    def echo_copy(part, strip):
        rows = pl.ds(strip * STRIP, STRIP)
        return pltpu.make_async_copy(
            echo_hbm.at[part, 0, rows], echo.at[part, rows], echo_sem.at[part, strip]
        )

    table_copies = [
        pltpu.make_async_copy(odd_hbm, odd, table_sem.at[0]),
        pltpu.make_async_copy(even_hbm, even, table_sem.at[1]),
    ]
    for strip in range(PULSES_DEV // STRIP):
        for part in range(2):
            echo_copy(part, strip).start()
    for copy in table_copies:
        copy.start()

    def put(folded, at, part, rows, left, values):
        high, low = split(values)
        cols = slice(left, left + values.shape[1])
        folded[at, part * 64 + rows : part * 64 + rows + 16, cols] = high
        folded[at, 128 + part * 64 + rows : 128 + part * 64 + rows + 16, cols] = low

    width = 256
    half = FOLD // 2
    for rows in range(0, PULSES_DEV, 16):
        if rows % STRIP == 0:
            for part in range(2):
                echo_copy(part, rows // STRIP).wait()
        for left in range(0, half, width):
            z = [[None] * 4 for _ in range(2)]
            for upper in range(2):
                at = left + upper * half
                pieces = [
                    [
                        echo[part, rows : rows + 16, a * FOLD + at : a * FOLD + at + width].astype(f32)
                        for a in range(RADIX)
                    ]
                    for part in range(2)
                ]
                (re0, re1, re2, re3), (im0, im1, im2, im3) = pieces
                re_s, re_t, im_s, im_t = re0 - re2, re1 - re3, im0 - im2, im1 - im3
                put(odd_sums, 0, 0, rows, at, re_s + im_t)
                put(odd_sums, 0, 1, rows, at, im_s - re_t)
                put(odd_sums, 1, 0, rows, at, re_s - im_t)
                put(odd_sums, 1, 1, rows, at, im_s + re_t)
                z[0][upper], z[0][2 + upper] = re0 + re2, re1 + re3
                z[1][upper], z[1][2 + upper] = im0 + im2, im1 + im3
            (re0, re1, re2, re3), (im0, im1, im2, im3) = z
            re_s, re_t, im_s, im_t = re0 + re2, re1 + re3, im0 + im2, im1 + im3
            put(even_sums, 0, 0, rows, left, re_s + re_t)
            put(even_sums, 0, 1, rows, left, im_s + im_t)
            put(even_sums, 2, 0, rows, left, re_s - re_t)
            put(even_sums, 2, 1, rows, left, im_s - im_t)
            re_s, re_t, im_s, im_t = re0 - re2, re1 - re3, im0 - im2, im1 - im3
            put(even_sums, 1, 0, rows, left, re_s + im_t)
            put(even_sums, 1, 1, rows, left, im_s - re_t)
            put(even_sums, 3, 0, rows, left, re_s - im_t)
            put(even_sums, 3, 1, rows, left, im_s + re_t)

    for copy in table_copies:
        copy.wait()
    zero_ref[...] = jnp.zeros((RB_DEV, LANES), f32)

    def transform(table, folded):
        sums = lax.dot_general(
            table, folded, (((1,), (1,)), ((), ())), preferred_element_type=f32
        )
        sums = sums[:, :LANES] + sums[:, LANES:]
        count = sums.shape[0] // 2
        sign = jnp.where(lane_index((count, LANES)) < 64, 1.0, -1.0)
        return sums[:count] + sign * pltpu.roll(sums[count:], 64, 1)

    for at in range(2):
        comp = transform(odd[at], odd_sums[at])
        for h in range(2):
            bins[pl.ds(4 * h + 2 * at + 1, N_PULSE, stride=RB_DEV), :] = comp[
                h * N_PULSE : (h + 1) * N_PULSE
            ]
    for e in range(4):
        bins[pl.ds(2 * e, N_PULSE, stride=RB_DEV), :] = transform(even[e], even_sums[e])
    own = bins[...].astype(bf16).reshape(N_PULSE // 2, 2, RB_DEV, LANES)
    odds, evens = own[:, 0], own[:, 1]
    edge = jnp.zeros((1, RB_DEV, LANES), bf16)
    last = N_PULSE // 2 - 1
    out_ref[:, 0, :, :LANES] = odds
    out_ref[0:1, 0, :, LANES:] = edge
    out_ref[1:, 0, :, LANES:] = evens[:last]
    out_ref[:last, 1, :, :LANES] = odds[1:]
    out_ref[last:, 1, :, :LANES] = edge
    out_ref[:, 1, :, LANES:] = evens


def compress(echoes, odd, even):
    windows, zeros = pl.pallas_call(
        compress_kernel,
        in_specs=[pl.BlockSpec(memory_space=pl.ANY)] * 3,
        out_shape=(
            jax.ShapeDtypeStruct((N_PULSE // 2, 2, RB_DEV, 2 * LANES), bf16),
            jax.ShapeDtypeStruct((RB_DEV, LANES), f32),
        ),
        scratch_shapes=[
            pltpu.VMEM((2, PULSES_DEV, NS), bf16),
            pltpu.VMEM((2, 256, FOLD), bf16),
            pltpu.VMEM((4, 128, FOLD // 2), bf16),
            pltpu.VMEM((2, 256, FOLD), bf16),
            pltpu.VMEM((4, 256, FOLD // 2), bf16),
            pltpu.VMEM((NR, LANES), f32),
            pltpu.SemaphoreType.DMA((2, PULSES_DEV // STRIP)),
            pltpu.SemaphoreType.DMA((2,)),
        ],
        compiler_params=pltpu.CompilerParams(vmem_limit_bytes=60 << 20),
        cost_estimate=pl.CostEstimate(
            flops=6 * 256 * 256 * FOLD, bytes_accessed=4 << 20, transcendentals=0
        ),
        name="compress",
    )(echoes, odd, even)
    return windows.reshape(N_PULSE, RB_DEV, 2 * LANES), zeros


def add(u, v):
    return (u[0] + v[0], u[1] + v[1])


def sub(u, v):
    return (u[0] - v[0], u[1] - v[1])


def times_i(u):
    return (-u[1], u[0])


def turn(u, angle):
    cos_a, sin_a = math.cos(angle), math.sin(angle)
    return (u[0] * cos_a - u[1] * sin_a, u[1] * cos_a + u[0] * sin_a)


def fft4(v0, v1, v2, v3):
    e0, e1 = add(v0, v2), sub(v0, v2)
    o0, o1 = add(v1, v3), times_i(sub(v1, v3))
    return [add(e0, o0), add(e1, o1), sub(e0, o0), sub(e1, o1)]


def fft8(values):
    half = math.sqrt(0.5)
    even = fft4(values[0], values[2], values[4], values[6])
    odd = fft4(values[1], values[3], values[5], values[7])
    odd[1] = ((odd[1][0] - odd[1][1]) * half, (odd[1][0] + odd[1][1]) * half)
    odd[2] = times_i(odd[2])
    odd[3] = ((-odd[3][0] - odd[3][1]) * half, (odd[3][0] - odd[3][1]) * half)
    return [add(e, o) for e, o in zip(even, odd)] + [sub(e, o) for e, o in zip(even, odd)]


def fft32(load, hold, store):
    for v in range(4):
        firsts = fft8([load(4 * u + v) for u in range(8)])
        for t in range(8):
            value = firsts[t]
            if t * v:
                value = turn(value, 2.0 * math.pi * t * v / 32)
            hold[0, v * 8 + t] = value[0]
            hold[1, v * 8 + t] = value[1]
    for t in range(8):
        seconds = fft4(*[(hold[0, v * 8 + t], hold[1, v * 8 + t]) for v in range(4)])
        for s in range(4):
            store(8 * s + t, seconds[s])


def spectra_kernel(turned_ref, lanes_ref, twiddle_ref, after_ref, out_ref, hold, samples):
    del after_ref
    low_half = lane_index((RB_DEV, LANES)) < 64
    table_hi, table_lo = lanes_ref[:, :256], lanes_ref[:, 256:]
    for group in range(2):
        cols = slice(group * LANES, (group + 1) * LANES)

        def load(p_hi):
            even = turned_ref[N_PULSE - 1 - 2 * p_hi, :, cols].astype(f32)
            odd = turned_ref[N_PULSE - 2 - 2 * p_hi, :, cols].astype(f32)
            real_x = jnp.where(low_half, even, pltpu.roll(odd, 64, 1))
            imag_x = jnp.where(low_half, pltpu.roll(even, 64, 1), odd)
            return (imag_x, real_x)

        def store(j_lo, value):
            imag_y, real_y = value
            rows = slice(j_lo * RB_DEV, (j_lo + 1) * RB_DEV)
            tw_re = twiddle_ref[group, rows, :LANES]
            tw_im = twiddle_ref[group, rows, LANES:]
            samples[group, rows, :LANES] = real_y * tw_re - imag_y * tw_im
            samples[group, rows, LANES:] = imag_y * tw_re + real_y * tw_im

        fft32(load, hold.at[group], store)
        high, low = split(samples[group])
        result = dot(high, table_hi) + (dot(low, table_hi) + dot(high, table_lo))
        out_ref[:, group * 16 : (group + 1) * 16, :] = result.astype(bf16).reshape(
            PAIR * CHANS, 16, 256
        )


def spectra(turned, lanes_table, twiddle, after):
    vmem = pl.BlockSpec(memory_space=pltpu.VMEM)
    return pl.pallas_call(
        spectra_kernel,
        in_specs=[vmem] * 3 + [pl.BlockSpec(memory_space=pl.ANY)],
        out_shape=jax.ShapeDtypeStruct((PAIR * CHANS, 32, 256), bf16),
        scratch_shapes=[
            pltpu.VMEM((2, 2, ROWS, RB_DEV, LANES), f32),
            pltpu.VMEM((2, 256, 256), f32),
        ],
        compiler_params=pltpu.CompilerParams(vmem_limit_bytes=32 << 20),
        cost_estimate=pl.CostEstimate(
            flops=4 * 256 * 256 * 768, bytes_accessed=2 << 20, transcendentals=0
        ),
        name="spectra",
    )(turned, lanes_table, twiddle, after)


def doppler_rows(scalars):
    block = scalars[CHANS + 1]
    member = jnp.bitwise_and(block, 1)
    shape = (OUT_ROWS, LANES)
    row = lax.broadcasted_iota(jnp.int32, shape, 0)
    lane = lax.broadcasted_iota(jnp.int32, shape, 1)
    digit = OWN * (LAST - member * CHANS - scalars[CHANS]) + lax.shift_right_logical(row, 4)
    bins = (block - member) * RB_DEV + jnp.bitwise_and(row, 15)
    return 32 * lane + digit, bins.astype(f32), jnp.bitwise_and(row, 7).astype(f32)


def doppler_of(band, doppler_bin):
    return (band * PULSES + doppler_bin).astype(f32) / SPECTRUM - 0.5


def tables_kernel(
    scalars,
    gain_ref,
    turns_ref,
    filter_ref,
    filt_ref,
    lanes_ref,
    twiddle_ref,
    base_ref,
    first_ref,
):
    chan = scalars[CHANS]
    first_digit = OWN * (LAST - jnp.bitwise_and(scalars[CHANS + 1], 1) * CHANS - chan)
    tw_cos = turns_ref[:, :LANES].reshape(ROWS, RB_DEV, LANES)
    tw_sin = turns_ref[:, LANES:].reshape(ROWS, RB_DEV, LANES)
    for group in range(2):
        gain_re, gain_im = gain_ref[0, group][None], gain_ref[1, group][None]
        first_ref[group, :, :LANES] = (gain_re * tw_cos + gain_im * tw_sin).reshape(256, LANES)
        first_ref[group, :, LANES:] = (gain_im * tw_cos - gain_re * tw_sin).reshape(256, LANES)
    doppler_bin, bins, q = doppler_rows(scalars)
    slope = 0.5 + 0.5 * bins / NR
    place = RB_DEV + q
    for k in range(CHANS):
        spread = 2.0 * jnp.square(2.0 * doppler_of(k, doppler_bin)) * slope - 1.0
        base_ref[k] = place - (place + MIGRATION * spread)
    pick_x = lax.broadcasted_iota(jnp.int32, (2048, LANES), 0)
    pick_y = lax.broadcasted_iota(jnp.int32, (2048, LANES), 1)
    wanted = 32 * jnp.bitwise_and(pick_y, 63) + first_digit + lax.shift_right_logical(pick_y, 6)
    pick = jnp.where(pick_x == wanted, 1.0, 0.0).astype(bf16)
    low_half = lane_index((128, LANES)) < 64
    left, right = [dot(filter_ref[:, 2048 * t : 2048 * (t + 1)], pick) for t in range(2)]
    filt_ref[0] = jnp.where(low_half, left, pltpu.roll(right, 64, 1))
    filt_ref[1] = jnp.where(low_half, pltpu.roll(left, 64, 1), right)
    square = (LANES, LANES)
    j_hi = lax.broadcasted_iota(jnp.int32, square, 0)
    m_lo = lax.broadcasted_iota(jnp.int32, square, 1)
    turns = jnp.bitwise_and(8 * j_hi * m_lo + j_hi * chan, 1023)
    angle = turns.astype(f32) * (2.0 * math.pi / 1024)
    cos_hi, cos_lo = split(jnp.cos(angle))
    sin_hi, sin_lo = split(jnp.sin(angle))
    for at, (cos_m, sin_m) in enumerate(((cos_hi, sin_hi), (cos_lo, sin_lo))):
        left, mid, right = 256 * at, 256 * at + LANES, 256 * at + 256
        lanes_ref[:LANES, left:mid] = cos_m
        lanes_ref[:LANES, mid:right] = sin_m
        lanes_ref[LANES:, left:mid] = -sin_m
        lanes_ref[LANES:, mid:right] = cos_m
    small = (ROWS, LANES)
    j_lo = lax.broadcasted_iota(jnp.int32, small, 0)
    m_low = lax.broadcasted_iota(jnp.int32, small, 1)
    angle = (j_lo * (8 * m_low + chan)).astype(f32) * (2.0 * math.pi / SPECTRUM)
    scale = 1.0 / math.sqrt(SPECTRUM)
    for at, values in enumerate((jnp.cos(angle) * scale, jnp.sin(angle) * scale)):
        full = jnp.broadcast_to(values[:, None, :], (ROWS, RB_DEV, LANES)).reshape(256, LANES)
        twiddle_ref[:, at * LANES : (at + 1) * LANES] = full


def tables(scalars, gain, turns, filters):
    vmem = pl.BlockSpec(memory_space=pltpu.VMEM)
    return pl.pallas_call(
        tables_kernel,
        in_specs=[pl.BlockSpec(memory_space=pltpu.SMEM)] + [vmem] * 3,
        out_shape=(
            jax.ShapeDtypeStruct((OWN, 128, LANES), f32),
            jax.ShapeDtypeStruct((256, 512), bf16),
            jax.ShapeDtypeStruct((256, 256), f32),
            jax.ShapeDtypeStruct((CHANS, OUT_ROWS, LANES), f32),
            jax.ShapeDtypeStruct((2, 256, 256), f32),
        ),
        compiler_params=pltpu.CompilerParams(vmem_limit_bytes=32 << 20),
        cost_estimate=pl.CostEstimate(
            flops=1 << 28, bytes_accessed=2 << 20, transcendentals=1 << 16
        ),
        name="tables",
    )(scalars, gain, turns, filters)


def phases_kernel(scalars, own_ref, other_ref, cos_ref, sin_ref, mask_ref):
    block = scalars[CHANS + 1]
    member = jnp.bitwise_and(block, 1)
    pair_start = (block - member) * RB_DEV
    own, other = own_ref[...], other_ref[...]
    given = [jnp.where(member == h, own, other) for h in range(PAIR)]
    shape = (RB_DEV, LANES)
    row = lax.broadcasted_iota(jnp.int32, shape, 0)
    for h in range(PAIR):
        low = jnp.broadcast_to(given[h][:, 64:65], shape)
        high = jnp.broadcast_to(given[h][:, 96:97], shape)
        for group in range(3):
            bins = (pair_start + (h + group - 1) * RB_DEV + row).astype(f32)
            inside = jnp.where(bins >= low, 1.0, 0.0) * jnp.where(bins < high, 1.0, 0.0)
            mask_ref[h, group] = inside
    doppler_bin = doppler_rows(scalars)[0]
    rates = [jnp.broadcast_to(given[h][:, 0:1], (RB_DEV, LANES)) for h in range(PAIR)]
    rates = jnp.concatenate(rates * OWN, axis=0)
    for k in range(CHANS):
        phase = -curvature * jnp.square(doppler_of(k, doppler_bin)) / rates
        cos_ref[k] = jnp.cos(phase)
        sin_ref[k] = jnp.sin(phase)


def phases(scalars, own, other):
    vmem = pl.BlockSpec(memory_space=pltpu.VMEM)
    rows = jax.ShapeDtypeStruct((CHANS, OUT_ROWS, LANES), f32)
    return pl.pallas_call(
        phases_kernel,
        in_specs=[pl.BlockSpec(memory_space=pltpu.SMEM)] + [vmem] * 2,
        out_shape=(
            rows,
            rows,
            jax.ShapeDtypeStruct((PAIR, 3, RB_DEV, LANES), f32),
        ),
        compiler_params=pltpu.CompilerParams(vmem_limit_bytes=32 << 20),
        cost_estimate=pl.CostEstimate(
            flops=1 << 24, bytes_accessed=1 << 20, transcendentals=1 << 18
        ),
        name="phases",
    )(scalars, own, other)


def band_steps(band):
    doppler = (band * PULSES + np.arange(PULSES)) / SPECTRUM - 0.5
    square = np.square(2.0 * doppler)
    lowest = MIGRATION * (2.0 * square.min() * 0.5 - 1.0) - 1e-3
    highest = MIGRATION * (2.0 * square.max() * (0.5 + 0.5 * (NR - 1) / NR) - 1.0) + 1e-3
    return range(max(-MIGRATION, math.floor(lowest)), min(MIGRATION, math.ceil(highest)) + 1)


def merge_kernel(
    scalars,
    gathered_ref,
    filt_ref,
    cos_ref,
    sin_ref,
    base_ref,
    mask_ref,
    out_ref,
    wide,
    merged,
    bands,
):
    wide[...] = gathered_ref[...].astype(f32)
    for band in range(CHANS):
        steps = band_steps(band)
        reach = [group for group, used in ((0, steps[0] < 0), (1, True), (2, steps[-1] > 0)) if used]
        needed = sorted({h + group for h in range(PAIR) for group in reach})
        first_row = pl.multiple_of(scalars[CHANS + 2 + band] * 16, 16)
        for digit in range(OWN):
            filters = filt_ref[digit, pl.ds(first_row, 16), :]
            sums_re = [None] * 4
            sums_im = [None] * 4
            for c in range(CHANS):
                f_re = jnp.broadcast_to(filters[2 * c : 2 * c + 1], (RB_DEV, LANES))
                f_im = jnp.broadcast_to(filters[2 * c + 1 : 2 * c + 2], (RB_DEV, LANES))
                for part in needed:
                    source = LAST - (part // 2) * CHANS - c
                    at = (part % 2) * 16 + digit * RB_DEV
                    s_re = wide[source, at : at + RB_DEV, :LANES]
                    s_im = wide[source, at : at + RB_DEV, LANES:]
                    part_re = f_re * s_re - f_im * s_im
                    part_im = f_re * s_im + f_im * s_re
                    sums_re[part] = part_re if c == 0 else sums_re[part] + part_re
                    sums_im[part] = part_im if c == 0 else sums_im[part] + part_im
            for h in range(PAIR):
                slot = ((band % 2) * OWN + digit) * PAIR + h
                for group in reach:
                    span = slice(group * RB_DEV, (group + 1) * RB_DEV)
                    inside = mask_ref[h, group]
                    merged[slot, 0, span, :] = sums_re[h + group] * inside
                    merged[slot, 1, span, :] = sums_im[h + group] * inside
                at = digit * PAIR * RB_DEV + h * RB_DEV
                rows = slice(at, at + RB_DEV)
                base = base_ref[band, rows, :]
                moved_re = moved_im = None
                for step in steps:
                    weight = jnp.maximum(0.0, 1.0 - jnp.abs(base + float(step)))
                    first = RB_DEV + step
                    part_re = weight * merged[slot, 0, first : first + RB_DEV, :]
                    part_im = weight * merged[slot, 1, first : first + RB_DEV, :]
                    moved_re = part_re if moved_re is None else moved_re + part_re
                    moved_im = part_im if moved_im is None else moved_im + part_im
                cos_p = cos_ref[band, rows, :]
                sin_p = sin_ref[band, rows, :]
                to = slice(digit * RB_DEV, (digit + 1) * RB_DEV)
                bands[band, 0, h, to, :] = moved_re * cos_p - moved_im * sin_p
                bands[band, 1, h, to, :] = moved_im * cos_p + moved_re * sin_p
    for h in range(PAIR):
        results = fft8([(bands[k, 0, h], bands[k, 1, h]) for k in range(CHANS)])
        for a in range(CHANS):
            out_ref[LAST - h * CHANS - a, :, :LANES] = results[a][0].astype(bf16)
            out_ref[LAST - h * CHANS - a, :, LANES:] = results[a][1].astype(bf16)


def merge(scalars, gathered, filt, cos_p, sin_p, base, mask):
    vmem = pl.BlockSpec(memory_space=pltpu.VMEM)
    return pl.pallas_call(
        merge_kernel,
        in_specs=[pl.BlockSpec(memory_space=pltpu.SMEM)] + [vmem] * 6,
        out_shape=jax.ShapeDtypeStruct((PAIR * CHANS, OWN * RB_DEV, 256), bf16),
        scratch_shapes=[
            pltpu.VMEM((PAIR * CHANS, 32, 256), f32),
            pltpu.VMEM((2 * OWN * PAIR, 2, 3 * RB_DEV, LANES), f32),
            pltpu.VMEM((CHANS, 2, PAIR, OWN * RB_DEV, LANES), f32),
        ],
        compiler_params=pltpu.CompilerParams(vmem_limit_bytes=32 << 20),
        cost_estimate=pl.CostEstimate(flops=1 << 24, bytes_accessed=2 << 20, transcendentals=0),
        name="merge",
    )(scalars, gathered, filt, cos_p, sin_p, base, mask)


def image_kernel(combined_ref, lanes_ref, twiddle_ref, out_ref, hold, samples):
    turned = dot(combined_ref[...].reshape(256, 256), lanes_ref[...])
    samples[...] = turned[:, :256] + turned[:, 256:]

    def load(j_lo):
        rows = slice(j_lo * RB_DEV, (j_lo + 1) * RB_DEV)
        real_y, imag_y = samples[rows, :LANES], samples[rows, LANES:]
        tw_cos, tw_sin = twiddle_ref[rows, :LANES], twiddle_ref[rows, LANES:]
        return (real_y * tw_cos - imag_y * tw_sin, imag_y * tw_cos + real_y * tw_sin)

    def store(m_hi, value):
        cols = slice(m_hi * LANES, (m_hi + 1) * LANES)
        out_ref[0, :, cols] = value[0]
        out_ref[1, :, cols] = value[1]

    fft32(load, hold, store)


def image(combined, lanes_table, twiddle):
    return pl.pallas_call(
        image_kernel,
        out_shape=jax.ShapeDtypeStruct((2, RB_DEV, PULSES), f32),
        scratch_shapes=[
            pltpu.VMEM((2, ROWS, RB_DEV, LANES), f32),
            pltpu.VMEM((256, 256), f32),
        ],
        compiler_params=pltpu.CompilerParams(vmem_limit_bytes=32 << 20),
        cost_estimate=pl.CostEstimate(
            flops=2 * 256 * 256 * 512, bytes_accessed=2 << 20, transcendentals=0
        ),
        name="image",
    )(combined, lanes_table, twiddle)


def window_gain(range_phase, first_bin):
    padded = jnp.pad(range_phase, (RB_DEV, RB_DEV))
    phase = lax.dynamic_slice(padded, (first_bin + RB_DEV,), (2 * RB_DEV,))
    scale = 1.0 / math.sqrt(NS * PULSES)
    gain = jnp.stack([scale * jnp.cos(phase), scale * jnp.sin(phase)])
    return jnp.broadcast_to(gain.reshape(2, 2, RB_DEV, 1), (2, 2, RB_DEV, LANES))


def block_values(azimuth_rate, band_lo, band_hi):
    return jnp.concatenate(
        [
            jnp.broadcast_to(azimuth_rate[:, None], (RB_DEV, 64)),
            jnp.broadcast_to(band_lo.astype(f32)[None, :], (RB_DEV, 32)),
            jnp.broadcast_to(band_hi.astype(f32)[None, :], (RB_DEV, 32)),
        ],
        axis=1,
    )


def per_device(echoes, range_phase, azimuth_rate, band_lo, band_hi, band_map, recon_filter):
    block_index = lax.axis_index("pulse").astype(jnp.int32)
    own_index = lax.axis_index("chan").astype(jnp.int32)
    order = lax.iota(jnp.int32, CHANS)
    row_of_band = jnp.sum(
        jnp.where(band_map[None, :] == order[:, None], order[None, :], 0), axis=1
    )
    scalars = jnp.concatenate([band_map, jnp.stack([own_index, block_index]), row_of_band])
    groups = [
        [(PAIR * i + h) * CHANS + d for h in range(PAIR) for d in range(CHANS)][::-1]
        for i in range(N_PULSE // PAIR)
    ]

    def exchange(values):
        return lax.all_to_all(
            values,
            ("pulse", "chan"),
            split_axis=0,
            concat_axis=0,
            axis_index_groups=groups,
            tiled=True,
        )

    windows, zeros = compress(echoes, jnp.asarray(odd_tables()), jnp.asarray(even_tables()))
    turned = lax.all_to_all(
        windows,
        "pulse",
        split_axis=0,
        concat_axis=0,
        axis_index_groups=[list(range(N_PULSE))[::-1]],
        tiled=True,
    )
    first_bin = (block_index - 1 + jnp.bitwise_and(block_index, 1)) * RB_DEV
    given = zeros + block_values(azimuth_rate, band_lo, band_hi)
    other = lax.ppermute(given, "pulse", [(b, b ^ 1) for b in range(N_PULSE)])
    filt, last_lanes, last_twiddle, base, first_twiddle = tables(
        scalars,
        window_gain(range_phase, first_bin),
        jnp.asarray(twiddle_tables()),
        recon_filter.reshape(2 * CHANS * CHANS, PULSES),
    )
    cos_p, sin_p, mask = phases(scalars, given, other)
    doppler = spectra(turned, jnp.asarray(lane_tables()), first_twiddle, mask)
    gathered = exchange(doppler)
    summed = merge(scalars, gathered, filt, cos_p, sin_p, base, mask)
    combined = exchange(summed)
    return image(combined, last_lanes, last_twiddle)


def solution(mesh):
    in_specs = (P(None, "chan", "pulse", None), P(), P("pulse"), P("pulse"), P("pulse"), P(), P())
    out_specs = P(None, "pulse", "chan")
    return jax.shard_map(
        per_device, mesh=mesh, in_specs=in_specs, out_specs=out_specs, check_vma=False
    )
```

```python
import math

import jax
import jax.numpy as jnp
import numpy as np
from jax import lax
from jax.experimental import pallas as pl
from jax.experimental.pallas import tpu as pltpu
from jax.sharding import PartitionSpec as P

NS = 4096
RB_DEV = 8
MIGRATION = 7
PULSES = 4096
NR = 512
CHANS = 8
SPECTRUM = 32768
N_PULSE = 64

RADIX = 4
FOLD = NS // RADIX
LANES = 128
ROWS = PULSES // LANES
PAIR = 2
LAST = PAIR * CHANS - 1
OWN = ROWS // (PAIR * CHANS)
OUT_ROWS = PAIR * RB_DEV * OWN
PULSES_DEV = PULSES // N_PULSE
STRIP = 32
FIRST = 62
BLOCK_ORDER = [(FIRST - g) % N_PULSE for g in range(N_PULSE)]
curvature = 300.0

f32 = jnp.float32
bf16 = jnp.bfloat16


def split_np(values):
    high = np.asarray(values, np.float32).astype(bf16)
    low = (values - high.astype(np.float64)).astype(np.float32).astype(bf16)
    return high, low


def range_table(bins, samples):
    angle = (np.asarray(bins)[:, None] * np.arange(samples)[None, :]) % NS * (2.0 * math.pi / NS)
    table = np.concatenate([np.cos(angle), np.sin(angle)], axis=0)
    return table.astype(np.float32).astype(bf16)


def odd_tables():
    blocks = RB_DEV * np.array(BLOCK_ORDER)
    return np.stack(
        [range_table(np.concatenate([blocks + r, blocks + 4 + r]), FOLD) for r in (1, 3)]
    )


def even_tables():
    blocks = RB_DEV * np.array(BLOCK_ORDER)
    return np.stack([range_table(blocks + 2 * e, FOLD // 2) for e in range(4)])


def lane_tables():
    digit = np.arange(LANES)
    angle = (digit[:, None] * digit[None, :]) % LANES * (2.0 * math.pi / LANES)
    cos_m, sin_m = np.cos(angle), np.sin(angle)
    high, low = split_np(np.block([[cos_m, -sin_m], [sin_m, cos_m]]))
    return np.concatenate([high, low], axis=1)


def twiddle_tables():
    angle = np.arange(ROWS)[:, None] * np.arange(LANES)[None, :] * (2.0 * math.pi / PULSES)
    angle = np.repeat(angle, RB_DEV, axis=0)
    return np.concatenate([np.cos(angle), np.sin(angle)], axis=1).astype(np.float32)


def dot(left, right):
    return jnp.dot(left, right, preferred_element_type=f32)


def split(values):
    high = values.astype(bf16)
    return high, (values - high.astype(f32)).astype(bf16)


def lane_index(shape):
    return lax.broadcasted_iota(jnp.int32, shape, 1)


def compress_kernel(
    echo_hbm,
    odd_hbm,
    even_hbm,
    out_ref,
    zero_ref,
    echo,
    odd,
    even,
    odd_sums,
    even_sums,
    bins,
    echo_sem,
    table_sem,
):
    def echo_copy(part, strip):
        rows = pl.ds(strip * STRIP, STRIP)
        return pltpu.make_async_copy(
            echo_hbm.at[part, 0, rows], echo.at[part, rows], echo_sem.at[part, strip]
        )

    table_copies = [
        pltpu.make_async_copy(odd_hbm, odd, table_sem.at[0]),
        pltpu.make_async_copy(even_hbm, even, table_sem.at[1]),
    ]
    for strip in range(PULSES_DEV // STRIP):
        for part in range(2):
            echo_copy(part, strip).start()
    for copy in table_copies:
        copy.start()

    def put(folded, at, part, rows, left, values):
        high, low = split(values)
        cols = slice(left, left + values.shape[1])
        folded[at, part * 64 + rows : part * 64 + rows + 16, cols] = high
        folded[at, 128 + part * 64 + rows : 128 + part * 64 + rows + 16, cols] = low

    width = 256
    half = FOLD // 2
    for rows in range(0, PULSES_DEV, 16):
        if rows % STRIP == 0:
            for part in range(2):
                echo_copy(part, rows // STRIP).wait()
        for left in range(0, half, width):
            z = [[None] * 4 for _ in range(2)]
            for upper in range(2):
                at = left + upper * half
                pieces = [
                    [
                        echo[part, rows : rows + 16, a * FOLD + at : a * FOLD + at + width].astype(f32)
                        for a in range(RADIX)
                    ]
                    for part in range(2)
                ]
                (re0, re1, re2, re3), (im0, im1, im2, im3) = pieces
                re_s, re_t, im_s, im_t = re0 - re2, re1 - re3, im0 - im2, im1 - im3
                put(odd_sums, 0, 0, rows, at, re_s + im_t)
                put(odd_sums, 0, 1, rows, at, im_s - re_t)
                put(odd_sums, 1, 0, rows, at, re_s - im_t)
                put(odd_sums, 1, 1, rows, at, im_s + re_t)
                z[0][upper], z[0][2 + upper] = re0 + re2, re1 + re3
                z[1][upper], z[1][2 + upper] = im0 + im2, im1 + im3
            (re0, re1, re2, re3), (im0, im1, im2, im3) = z
            re_s, re_t, im_s, im_t = re0 + re2, re1 + re3, im0 + im2, im1 + im3
            put(even_sums, 0, 0, rows, left, re_s + re_t)
            put(even_sums, 0, 1, rows, left, im_s + im_t)
            put(even_sums, 2, 0, rows, left, re_s - re_t)
            put(even_sums, 2, 1, rows, left, im_s - im_t)
            re_s, re_t, im_s, im_t = re0 - re2, re1 - re3, im0 - im2, im1 - im3
            put(even_sums, 1, 0, rows, left, re_s + im_t)
            put(even_sums, 1, 1, rows, left, im_s - re_t)
            put(even_sums, 3, 0, rows, left, re_s - im_t)
            put(even_sums, 3, 1, rows, left, im_s + re_t)

    for copy in table_copies:
        copy.wait()
    zero_ref[...] = jnp.zeros((RB_DEV, LANES), f32)

    def transform(table, folded):
        sums = lax.dot_general(
            table, folded, (((1,), (1,)), ((), ())), preferred_element_type=f32
        )
        sums = sums[:, :LANES] + sums[:, LANES:]
        count = sums.shape[0] // 2
        sign = jnp.where(lane_index((count, LANES)) < 64, 1.0, -1.0)
        return sums[:count] + sign * pltpu.roll(sums[count:], 64, 1)

    for at in range(2):
        comp = transform(odd[at], odd_sums[at])
        for h in range(2):
            bins[pl.ds(4 * h + 2 * at + 1, N_PULSE, stride=RB_DEV), :] = comp[
                h * N_PULSE : (h + 1) * N_PULSE
            ]
    for e in range(4):
        bins[pl.ds(2 * e, N_PULSE, stride=RB_DEV), :] = transform(even[e], even_sums[e])
    own = bins[...].astype(bf16).reshape(N_PULSE // 2, 2, RB_DEV, LANES)
    evens, odds = own[:, 0], own[:, 1]
    edge = jnp.zeros((RB_DEV, LANES), bf16)
    for member in range(2):
        out_ref[:, member, :, :LANES] = odds
        out_ref[:, member, :, LANES:] = evens
    out_ref[FIRST // 2, 0, :, :LANES] = edge
    out_ref[FIRST // 2, 1, :, LANES:] = edge


def compress(echoes, odd, even):
    windows, zeros = pl.pallas_call(
        compress_kernel,
        in_specs=[pl.BlockSpec(memory_space=pl.ANY)] * 3,
        out_shape=(
            jax.ShapeDtypeStruct((N_PULSE // 2, 2, RB_DEV, 2 * LANES), bf16),
            jax.ShapeDtypeStruct((RB_DEV, LANES), f32),
        ),
        scratch_shapes=[
            pltpu.VMEM((2, PULSES_DEV, NS), bf16),
            pltpu.VMEM((2, 256, FOLD), bf16),
            pltpu.VMEM((4, 128, FOLD // 2), bf16),
            pltpu.VMEM((2, 256, FOLD), bf16),
            pltpu.VMEM((4, 256, FOLD // 2), bf16),
            pltpu.VMEM((NR, LANES), f32),
            pltpu.SemaphoreType.DMA((2, PULSES_DEV // STRIP)),
            pltpu.SemaphoreType.DMA((2,)),
        ],
        compiler_params=pltpu.CompilerParams(vmem_limit_bytes=60 << 20),
        cost_estimate=pl.CostEstimate(
            flops=6 * 256 * 256 * FOLD, bytes_accessed=4 << 20, transcendentals=0
        ),
        name="compress",
    )(echoes, odd, even)
    return windows.reshape(N_PULSE, RB_DEV, 2 * LANES), zeros


def add(u, v):
    return (u[0] + v[0], u[1] + v[1])


def sub(u, v):
    return (u[0] - v[0], u[1] - v[1])


def times_i(u):
    return (-u[1], u[0])


def turn(u, angle):
    cos_a, sin_a = math.cos(angle), math.sin(angle)
    return (u[0] * cos_a - u[1] * sin_a, u[1] * cos_a + u[0] * sin_a)


def fft4(v0, v1, v2, v3):
    e0, e1 = add(v0, v2), sub(v0, v2)
    o0, o1 = add(v1, v3), times_i(sub(v1, v3))
    return [add(e0, o0), add(e1, o1), sub(e0, o0), sub(e1, o1)]


def fft8(values):
    half = math.sqrt(0.5)
    even = fft4(values[0], values[2], values[4], values[6])
    odd = fft4(values[1], values[3], values[5], values[7])
    odd[1] = ((odd[1][0] - odd[1][1]) * half, (odd[1][0] + odd[1][1]) * half)
    odd[2] = times_i(odd[2])
    odd[3] = ((-odd[3][0] - odd[3][1]) * half, (odd[3][0] - odd[3][1]) * half)
    return [add(e, o) for e, o in zip(even, odd)] + [sub(e, o) for e, o in zip(even, odd)]


def fft32(load, hold, store):
    for v in range(4):
        firsts = fft8([load(4 * u + v) for u in range(8)])
        for t in range(8):
            value = firsts[t]
            if t * v:
                value = turn(value, 2.0 * math.pi * t * v / 32)
            hold[0, v * 8 + t] = value[0]
            hold[1, v * 8 + t] = value[1]
    for t in range(8):
        seconds = fft4(*[(hold[0, v * 8 + t], hold[1, v * 8 + t]) for v in range(4)])
        for s in range(4):
            store(8 * s + t, seconds[s])


def spectra_kernel(turned_ref, lanes_ref, twiddle_ref, after_ref, out_ref, hold, samples):
    del after_ref
    low_half = lane_index((RB_DEV, LANES)) < 64
    table_hi, table_lo = lanes_ref[:, :256], lanes_ref[:, 256:]
    for group in range(2):
        cols = slice(group * LANES, (group + 1) * LANES)

        def load(p_hi):
            even = turned_ref[(FIRST - 2 * p_hi) % N_PULSE, :, cols].astype(f32)
            odd = turned_ref[(FIRST - 2 * p_hi - 1) % N_PULSE, :, cols].astype(f32)
            real_x = jnp.where(low_half, even, pltpu.roll(odd, 64, 1))
            imag_x = jnp.where(low_half, pltpu.roll(even, 64, 1), odd)
            return (imag_x, real_x)

        def store(j_lo, value):
            imag_y, real_y = value
            rows = slice(j_lo * RB_DEV, (j_lo + 1) * RB_DEV)
            tw_re = twiddle_ref[group, rows, :LANES]
            tw_im = twiddle_ref[group, rows, LANES:]
            samples[group, rows, :LANES] = real_y * tw_re - imag_y * tw_im
            samples[group, rows, LANES:] = imag_y * tw_re + real_y * tw_im

        fft32(load, hold.at[group], store)
        high, low = split(samples[group])
        result = dot(high, table_hi) + (dot(low, table_hi) + dot(high, table_lo))
        out_ref[:, group * 16 : (group + 1) * 16, :] = result.astype(bf16).reshape(
            PAIR * CHANS, 16, 256
        )


def spectra(turned, lanes_table, twiddle, after):
    vmem = pl.BlockSpec(memory_space=pltpu.VMEM)
    return pl.pallas_call(
        spectra_kernel,
        in_specs=[vmem] * 3 + [pl.BlockSpec(memory_space=pl.ANY)],
        out_shape=jax.ShapeDtypeStruct((PAIR * CHANS, 32, 256), bf16),
        scratch_shapes=[
            pltpu.VMEM((2, 2, ROWS, RB_DEV, LANES), f32),
            pltpu.VMEM((2, 256, 256), f32),
        ],
        compiler_params=pltpu.CompilerParams(vmem_limit_bytes=32 << 20),
        cost_estimate=pl.CostEstimate(
            flops=4 * 256 * 256 * 768, bytes_accessed=2 << 20, transcendentals=0
        ),
        name="spectra",
    )(turned, lanes_table, twiddle, after)


def doppler_rows(scalars):
    block = scalars[CHANS + 1]
    member = jnp.bitwise_and(block, 1)
    shape = (OUT_ROWS, LANES)
    row = lax.broadcasted_iota(jnp.int32, shape, 0)
    lane = lax.broadcasted_iota(jnp.int32, shape, 1)
    digit = OWN * (LAST - member * CHANS - scalars[CHANS]) + lax.shift_right_logical(row, 4)
    bins = (block - member) * RB_DEV + jnp.bitwise_and(row, 15)
    return 32 * lane + digit, bins.astype(f32), jnp.bitwise_and(row, 7).astype(f32)


def doppler_of(band, doppler_bin):
    return (band * PULSES + doppler_bin).astype(f32) / SPECTRUM - 0.5


def tables_kernel(
    scalars,
    gain_ref,
    turns_ref,
    filter_ref,
    filt_ref,
    lanes_ref,
    twiddle_ref,
    base_ref,
    first_ref,
):
    chan = scalars[CHANS]
    first_digit = OWN * (LAST - jnp.bitwise_and(scalars[CHANS + 1], 1) * CHANS - chan)
    tw_cos = turns_ref[:, :LANES].reshape(ROWS, RB_DEV, LANES)
    tw_sin = turns_ref[:, LANES:].reshape(ROWS, RB_DEV, LANES)
    for group in range(2):
        gain_re, gain_im = gain_ref[0, group][None], gain_ref[1, group][None]
        first_ref[group, :, :LANES] = (gain_re * tw_cos + gain_im * tw_sin).reshape(256, LANES)
        first_ref[group, :, LANES:] = (gain_im * tw_cos - gain_re * tw_sin).reshape(256, LANES)
    doppler_bin, bins, q = doppler_rows(scalars)
    slope = 0.5 + 0.5 * bins / NR
    place = RB_DEV + q
    for k in range(CHANS):
        spread = 2.0 * jnp.square(2.0 * doppler_of(k, doppler_bin)) * slope - 1.0
        base_ref[k] = place - (place + MIGRATION * spread)
    pick_x = lax.broadcasted_iota(jnp.int32, (2048, LANES), 0)
    pick_y = lax.broadcasted_iota(jnp.int32, (2048, LANES), 1)
    wanted = 32 * jnp.bitwise_and(pick_y, 63) + first_digit + lax.shift_right_logical(pick_y, 6)
    pick = jnp.where(pick_x == wanted, 1.0, 0.0).astype(bf16)
    low_half = lane_index((128, LANES)) < 64
    left, right = [dot(filter_ref[:, 2048 * t : 2048 * (t + 1)], pick) for t in range(2)]
    filt_ref[0] = jnp.where(low_half, left, pltpu.roll(right, 64, 1))
    filt_ref[1] = jnp.where(low_half, pltpu.roll(left, 64, 1), right)
    square = (LANES, LANES)
    j_hi = lax.broadcasted_iota(jnp.int32, square, 0)
    m_lo = lax.broadcasted_iota(jnp.int32, square, 1)
    turns = jnp.bitwise_and(8 * j_hi * m_lo + j_hi * chan, 1023)
    angle = turns.astype(f32) * (2.0 * math.pi / 1024)
    cos_hi, cos_lo = split(jnp.cos(angle))
    sin_hi, sin_lo = split(jnp.sin(angle))
    for at, (cos_m, sin_m) in enumerate(((cos_hi, sin_hi), (cos_lo, sin_lo))):
        left, mid, right = 256 * at, 256 * at + LANES, 256 * at + 256
        lanes_ref[:LANES, left:mid] = cos_m
        lanes_ref[:LANES, mid:right] = sin_m
        lanes_ref[LANES:, left:mid] = -sin_m
        lanes_ref[LANES:, mid:right] = cos_m
    small = (ROWS, LANES)
    j_lo = lax.broadcasted_iota(jnp.int32, small, 0)
    m_low = lax.broadcasted_iota(jnp.int32, small, 1)
    angle = (j_lo * (8 * m_low + chan)).astype(f32) * (2.0 * math.pi / SPECTRUM)
    scale = 1.0 / math.sqrt(SPECTRUM)
    for at, values in enumerate((jnp.cos(angle) * scale, jnp.sin(angle) * scale)):
        full = jnp.broadcast_to(values[:, None, :], (ROWS, RB_DEV, LANES)).reshape(256, LANES)
        twiddle_ref[:, at * LANES : (at + 1) * LANES] = full


def tables(scalars, gain, turns, filters):
    vmem = pl.BlockSpec(memory_space=pltpu.VMEM)
    return pl.pallas_call(
        tables_kernel,
        in_specs=[pl.BlockSpec(memory_space=pltpu.SMEM)] + [vmem] * 3,
        out_shape=(
            jax.ShapeDtypeStruct((OWN, 128, LANES), f32),
            jax.ShapeDtypeStruct((256, 512), bf16),
            jax.ShapeDtypeStruct((256, 256), f32),
            jax.ShapeDtypeStruct((CHANS, OUT_ROWS, LANES), f32),
            jax.ShapeDtypeStruct((2, 256, 256), f32),
        ),
        compiler_params=pltpu.CompilerParams(vmem_limit_bytes=32 << 20),
        cost_estimate=pl.CostEstimate(
            flops=1 << 28, bytes_accessed=2 << 20, transcendentals=1 << 16
        ),
        name="tables",
    )(scalars, gain, turns, filters)


def phases_kernel(scalars, own_ref, other_ref, cos_ref, sin_ref, mask_ref):
    block = scalars[CHANS + 1]
    member = jnp.bitwise_and(block, 1)
    pair_start = (block - member) * RB_DEV
    own, other = own_ref[...], other_ref[...]
    given = [jnp.where(member == h, own, other) for h in range(PAIR)]
    shape = (RB_DEV, LANES)
    row = lax.broadcasted_iota(jnp.int32, shape, 0)
    for h in range(PAIR):
        low = jnp.broadcast_to(given[h][:, 64:65], shape)
        high = jnp.broadcast_to(given[h][:, 96:97], shape)
        for group in range(3):
            bins = (pair_start + (h + group - 1) * RB_DEV + row).astype(f32)
            inside = jnp.where(bins >= low, 1.0, 0.0) * jnp.where(bins < high, 1.0, 0.0)
            mask_ref[h, group] = inside
    doppler_bin = doppler_rows(scalars)[0]
    rates = [jnp.broadcast_to(given[h][:, 0:1], (RB_DEV, LANES)) for h in range(PAIR)]
    rates = jnp.concatenate(rates * OWN, axis=0)
    for k in range(CHANS):
        phase = -curvature * jnp.square(doppler_of(k, doppler_bin)) / rates
        cos_ref[k] = jnp.cos(phase)
        sin_ref[k] = jnp.sin(phase)


def phases(scalars, own, other):
    vmem = pl.BlockSpec(memory_space=pltpu.VMEM)
    rows = jax.ShapeDtypeStruct((CHANS, OUT_ROWS, LANES), f32)
    return pl.pallas_call(
        phases_kernel,
        in_specs=[pl.BlockSpec(memory_space=pltpu.SMEM)] + [vmem] * 2,
        out_shape=(
            rows,
            rows,
            jax.ShapeDtypeStruct((PAIR, 3, RB_DEV, LANES), f32),
        ),
        compiler_params=pltpu.CompilerParams(vmem_limit_bytes=32 << 20),
        cost_estimate=pl.CostEstimate(
            flops=1 << 24, bytes_accessed=1 << 20, transcendentals=1 << 18
        ),
        name="phases",
    )(scalars, own, other)


def band_steps(band):
    doppler = (band * PULSES + np.arange(PULSES)) / SPECTRUM - 0.5
    square = np.square(2.0 * doppler)
    lowest = MIGRATION * (2.0 * square.min() * 0.5 - 1.0) - 1e-3
    highest = MIGRATION * (2.0 * square.max() * (0.5 + 0.5 * (NR - 1) / NR) - 1.0) + 1e-3
    return range(max(-MIGRATION, math.floor(lowest)), min(MIGRATION, math.ceil(highest)) + 1)


def merge_kernel(
    scalars,
    gathered_ref,
    filt_ref,
    cos_ref,
    sin_ref,
    base_ref,
    mask_ref,
    out_ref,
    wide,
    merged,
    bands,
):
    wide[...] = gathered_ref[...].astype(f32)
    for band in range(CHANS):
        steps = band_steps(band)
        reach = [group for group, used in ((0, steps[0] < 0), (1, True), (2, steps[-1] > 0)) if used]
        needed = sorted({h + group for h in range(PAIR) for group in reach})
        first_row = pl.multiple_of(scalars[CHANS + 2 + band] * 16, 16)
        for digit in range(OWN):
            filters = filt_ref[digit, pl.ds(first_row, 16), :]
            sums_re = [None] * 4
            sums_im = [None] * 4
            for c in range(CHANS):
                f_re = jnp.broadcast_to(filters[2 * c : 2 * c + 1], (RB_DEV, LANES))
                f_im = jnp.broadcast_to(filters[2 * c + 1 : 2 * c + 2], (RB_DEV, LANES))
                for part in needed:
                    source = LAST - (part // 2) * CHANS - c
                    at = (part % 2) * 16 + digit * RB_DEV
                    s_re = wide[source, at : at + RB_DEV, :LANES]
                    s_im = wide[source, at : at + RB_DEV, LANES:]
                    part_re = f_re * s_re - f_im * s_im
                    part_im = f_re * s_im + f_im * s_re
                    sums_re[part] = part_re if c == 0 else sums_re[part] + part_re
                    sums_im[part] = part_im if c == 0 else sums_im[part] + part_im
            for h in range(PAIR):
                slot = ((band % 2) * OWN + digit) * PAIR + h
                for group in reach:
                    span = slice(group * RB_DEV, (group + 1) * RB_DEV)
                    inside = mask_ref[h, group]
                    merged[slot, 0, span, :] = sums_re[h + group] * inside
                    merged[slot, 1, span, :] = sums_im[h + group] * inside
                at = digit * PAIR * RB_DEV + h * RB_DEV
                rows = slice(at, at + RB_DEV)
                base = base_ref[band, rows, :]
                moved_re = moved_im = None
                for step in steps:
                    weight = jnp.maximum(0.0, 1.0 - jnp.abs(base + float(step)))
                    first = RB_DEV + step
                    part_re = weight * merged[slot, 0, first : first + RB_DEV, :]
                    part_im = weight * merged[slot, 1, first : first + RB_DEV, :]
                    moved_re = part_re if moved_re is None else moved_re + part_re
                    moved_im = part_im if moved_im is None else moved_im + part_im
                cos_p = cos_ref[band, rows, :]
                sin_p = sin_ref[band, rows, :]
                to = slice(digit * RB_DEV, (digit + 1) * RB_DEV)
                bands[band, 0, h, to, :] = moved_re * cos_p - moved_im * sin_p
                bands[band, 1, h, to, :] = moved_im * cos_p + moved_re * sin_p
    for h in range(PAIR):
        results = fft8([(bands[k, 0, h], bands[k, 1, h]) for k in range(CHANS)])
        for a in range(CHANS):
            out_ref[LAST - h * CHANS - a, :, :LANES] = results[a][0].astype(bf16)
            out_ref[LAST - h * CHANS - a, :, LANES:] = results[a][1].astype(bf16)


def merge(scalars, gathered, filt, cos_p, sin_p, base, mask):
    vmem = pl.BlockSpec(memory_space=pltpu.VMEM)
    return pl.pallas_call(
        merge_kernel,
        in_specs=[pl.BlockSpec(memory_space=pltpu.SMEM)] + [vmem] * 6,
        out_shape=jax.ShapeDtypeStruct((PAIR * CHANS, OWN * RB_DEV, 256), bf16),
        scratch_shapes=[
            pltpu.VMEM((PAIR * CHANS, 32, 256), f32),
            pltpu.VMEM((2 * OWN * PAIR, 2, 3 * RB_DEV, LANES), f32),
            pltpu.VMEM((CHANS, 2, PAIR, OWN * RB_DEV, LANES), f32),
        ],
        compiler_params=pltpu.CompilerParams(vmem_limit_bytes=32 << 20),
        cost_estimate=pl.CostEstimate(flops=1 << 24, bytes_accessed=2 << 20, transcendentals=0),
        name="merge",
    )(scalars, gathered, filt, cos_p, sin_p, base, mask)


def image_kernel(combined_ref, lanes_ref, twiddle_ref, out_ref, hold, samples):
    turned = dot(combined_ref[...].reshape(256, 256), lanes_ref[...])
    samples[...] = turned[:, :256] + turned[:, 256:]

    def load(j_lo):
        rows = slice(j_lo * RB_DEV, (j_lo + 1) * RB_DEV)
        real_y, imag_y = samples[rows, :LANES], samples[rows, LANES:]
        tw_cos, tw_sin = twiddle_ref[rows, :LANES], twiddle_ref[rows, LANES:]
        return (real_y * tw_cos - imag_y * tw_sin, imag_y * tw_cos + real_y * tw_sin)

    def store(m_hi, value):
        cols = slice(m_hi * LANES, (m_hi + 1) * LANES)
        out_ref[0, :, cols] = value[0]
        out_ref[1, :, cols] = value[1]

    fft32(load, hold, store)


def image(combined, lanes_table, twiddle):
    return pl.pallas_call(
        image_kernel,
        out_shape=jax.ShapeDtypeStruct((2, RB_DEV, PULSES), f32),
        scratch_shapes=[
            pltpu.VMEM((2, ROWS, RB_DEV, LANES), f32),
            pltpu.VMEM((256, 256), f32),
        ],
        compiler_params=pltpu.CompilerParams(vmem_limit_bytes=32 << 20),
        cost_estimate=pl.CostEstimate(
            flops=2 * 256 * 256 * 512, bytes_accessed=2 << 20, transcendentals=0
        ),
        name="image",
    )(combined, lanes_table, twiddle)


def window_gain(range_phase, first_bin):
    padded = jnp.pad(range_phase, (RB_DEV, RB_DEV))
    phase = lax.dynamic_slice(padded, (first_bin + RB_DEV,), (2 * RB_DEV,))
    scale = 1.0 / math.sqrt(NS * PULSES)
    gain = jnp.stack([scale * jnp.cos(phase), scale * jnp.sin(phase)])
    return jnp.broadcast_to(gain.reshape(2, 2, RB_DEV, 1), (2, 2, RB_DEV, LANES))


def block_values(azimuth_rate, band_lo, band_hi):
    return jnp.concatenate(
        [
            jnp.broadcast_to(azimuth_rate[:, None], (RB_DEV, 64)),
            jnp.broadcast_to(band_lo.astype(f32)[None, :], (RB_DEV, 32)),
            jnp.broadcast_to(band_hi.astype(f32)[None, :], (RB_DEV, 32)),
        ],
        axis=1,
    )


def per_device(echoes, range_phase, azimuth_rate, band_lo, band_hi, band_map, recon_filter):
    block_index = lax.axis_index("pulse").astype(jnp.int32)
    own_index = lax.axis_index("chan").astype(jnp.int32)
    order = lax.iota(jnp.int32, CHANS)
    row_of_band = jnp.sum(
        jnp.where(band_map[None, :] == order[:, None], order[None, :], 0), axis=1
    )
    scalars = jnp.concatenate([band_map, jnp.stack([own_index, block_index]), row_of_band])
    groups = [
        [(PAIR * i + h) * CHANS + d for h in range(PAIR) for d in range(CHANS)][::-1]
        for i in range(N_PULSE // PAIR)
    ]

    def exchange(values):
        return lax.all_to_all(
            values,
            ("pulse", "chan"),
            split_axis=0,
            concat_axis=0,
            axis_index_groups=groups,
            tiled=True,
        )

    windows, zeros = compress(echoes, jnp.asarray(odd_tables()), jnp.asarray(even_tables()))
    turned = lax.all_to_all(
        windows,
        "pulse",
        split_axis=0,
        concat_axis=0,
        axis_index_groups=[BLOCK_ORDER],
        tiled=True,
    )
    first_bin = (block_index - 1 + jnp.bitwise_and(block_index, 1)) * RB_DEV
    given = zeros + block_values(azimuth_rate, band_lo, band_hi)
    other = lax.ppermute(given, "pulse", [(b, b ^ 1) for b in range(N_PULSE)])
    filt, last_lanes, last_twiddle, base, first_twiddle = tables(
        scalars,
        window_gain(range_phase, first_bin),
        jnp.asarray(twiddle_tables()),
        recon_filter.reshape(2 * CHANS * CHANS, PULSES),
    )
    cos_p, sin_p, mask = phases(scalars, given, other)
    doppler = spectra(turned, jnp.asarray(lane_tables()), first_twiddle, mask)
    gathered = exchange(doppler)
    summed = merge(scalars, gathered, filt, cos_p, sin_p, base, mask)
    combined = exchange(summed)
    return image(combined, last_lanes, last_twiddle)


def solution(mesh):
    in_specs = (P(None, "chan", "pulse", None), P(), P("pulse"), P("pulse"), P("pulse"), P(), P())
    out_specs = P(None, "pulse", "chan")
    return jax.shard_map(
        per_device, mesh=mesh, in_specs=in_specs, out_specs=out_specs, check_vma=False
    )
```
